32 devices in a mesh: exp: 8 (over z, y), row: 4 (over x, core).
Axes of the slice: x: 2, y: 2, z: 4, core: 2. Of those that a mesh axis runs over, the one named last changes fastest.
Arguments:
- latent: bfloat16 [4, 1024, 1024], P(None, 'row', 'exp'), may hold values from -6 to 6
- row_taps: bfloat16 [16, 21], replicated, may hold values from -1.25 to 1.25
- column_taps: bfloat16 [16, 21], replicated, may hold values from -1.25 to 1.25
- coefficients: bfloat16 [8, 16, 1024, 1024], P('exp', None, 'row'), may hold values from -1.5 to 1.5
- observed: bfloat16 [8, 1024, 1024], P('exp', 'row'), may hold values from -6 to 6
- cell_of: int32 [8, 1], replicated, may hold values from 0 to 3
- valid_rows: int32 [8, 1024], P('exp', 'row'), may hold values 0 or 1
Outputs:
- gradient: float32 [4, 1024, 1024], P(None, 'row', 'exp')
- residuals: float32 [8, 1024, 1024], P('exp', 'row')
The draws below stay inside these ranges and needn't reach their ends.
Inputs may be any that keep to these rules, and one draw needn't show every extreme that they name: `cell_of`: every sky cell is covered by at least one exposure.
All inputs are finite; a program needn't handle non-finite values. No bound on the sum of `valid_rows` on one device may be relied on, other than what follows from the above.
Results may differ from the reference program's by a relative error of at most 0.0023.
Values may be sent and summed in bfloat16 or wider, within the bound.
A program may use at most 128 MiB of HBM per device.

```python
import jax
import jax.numpy as jnp
from jax import lax

KERNELS = 16
TAPS = 21
CELLS = 4
COLS = 1024
CELL_ROWS = 1024
EXPOSURES = 8


def with_ends(drawn, stream_key, low, top_value):
    spot = [jax.random.randint(jax.random.fold_in(stream_key, axis), (), 0, length) for axis, length in enumerate(drawn.shape)]
    main_axis = drawn.shape.index(max(drawn.shape))
    neighbour = spot[:main_axis] + [(spot[main_axis] + 1) % drawn.shape[main_axis]] + spot[main_axis + 1:]
    return drawn.at[tuple(spot)].set(low).at[tuple(neighbour)].set(top_value)


def shard_levels(rng, extent, cuts, low, high):
    loudness, own = 1.0, jax.random.fold_in(rng, 6)
    for axis_at, blocks in cuts:
        steps = jnp.exp(jax.random.uniform(jax.random.fold_in(own, axis_at), (blocks,), jnp.float32, low / len(cuts), high / len(cuts)))
        loudness = loudness * jnp.repeat(steps, extent[axis_at] // blocks).reshape([-1 if axis == axis_at else 1 for axis in range(len(extent))])
    return loudness


def choose_distinct(rng, rows, number_of, top, lift):
    ranking = jax.random.permutation(jax.random.fold_in(rng, 1), number_of)
    pull = ranking
    for power in range(3):
        pull = pull * pull // number_of
    pull = pull * lift // number_of
    chance = jax.random.randint(jax.random.fold_in(rng, 2), (rows, number_of), 0, 4096) + pull
    sure = jax.random.permutation(jax.random.fold_in(rng, 3), rows)[jnp.arange(number_of) % rows]
    chance = jnp.where(jnp.arange(rows)[:, None] == sure[None, :], 1 << 14, chance)
    priority = chance * number_of + jnp.arange(number_of)
    return lax.top_k(priority.astype(jnp.int32), top)[1].astype(jnp.int32)


def gaussian(own_key, shape, spread, reach, shards=(), held_as=jnp.bfloat16):
    drawn = jax.random.normal(own_key, shape, jnp.float32) * spread
    if len(shards) > 0:
        drawn = shard_levels(own_key, shape, shards, -0.22, 0.18) * drawn
    return jnp.clip(drawn, min=-reach, max=reach).astype(held_as)


def setup_inputs(seed: int = 0) -> dict:
    key_of = jax.random.split(jax.random.key(seed), 8)
    return {
        "latent": gaussian(key_of[0], (CELLS, CELL_ROWS, COLS), 1.0, 6.0, ((1, 4), (2, 8))),
        "row_taps": gaussian(key_of[1], (KERNELS, TAPS), TAPS ** -0.5, 1.25),
        "column_taps": gaussian(key_of[2], (KERNELS, TAPS), TAPS ** -0.5, 1.25),
        "coefficients": gaussian(key_of[3], (EXPOSURES, KERNELS, CELL_ROWS, COLS), 0.25, 1.5, ((0, 8), (2, 4))),
        "observed": gaussian(key_of[4], (EXPOSURES, CELL_ROWS, COLS), 1.0, 6.0, ((0, 8), (1, 4))),
        "cell_of": choose_distinct(key_of[5], EXPOSURES, CELLS, 1, 2048),
        "valid_rows": with_ends((jax.random.randint(key_of[6], (EXPOSURES, CELL_ROWS), 0, 8) < 7).astype(jnp.int32), jax.random.fold_in(key_of[6], 1), 0, 1),
    }


def bands(kernel_taps, adjoint):
    tap_count = kernel_taps.shape[1]
    halfwidth = tap_count // 2
    inputs_at = jnp.arange(384)[:, None]
    outputs_at = jnp.arange(128)[None, :]
    if adjoint:
        offset = outputs_at - inputs_at + 128 + halfwidth
    else:
        offset = inputs_at - 128 - outputs_at + halfwidth
    onehot = (offset[:, :, None] == jnp.arange(tap_count)[None, None, :]).astype(jnp.float32)
    return jnp.einsum('kt,pqt->kpq', kernel_taps.astype(jnp.float32), onehot)


def stacked_blocks(source):
    length = source.shape[-1]
    nblocks = length // 128
    padding = [(0, 0)] * (source.ndim - 1) + [(128, 128)]
    padded = jnp.pad(source, padding)
    blocked = padded.reshape(source.shape[:-1] + (nblocks + 2, 128))
    return jnp.concatenate([blocked[..., :-2, :], blocked[..., 1:-1, :], blocked[..., 2:, :]], axis=-1)


def filter_last(source, band_table):
    stacked = stacked_blocks(source)
    result = jnp.einsum('kabp,kpq->kabq', stacked, band_table)
    return result.reshape(source.shape)


def reference(latent, row_taps, column_taps, coefficients, observed, cell_of, valid_rows):
    forward_row = bands(row_taps, False)
    forward_col = bands(column_taps, False)
    adjoint_row = bands(row_taps, True)
    adjoint_col = bands(column_taps, True)
    kernel_count = row_taps.shape[0]
    cell_count = latent.shape[0]

    def blur_cell(image):
        stacked = stacked_blocks(image.astype(jnp.float32))
        result = jnp.einsum('abp,kpq->kabq', stacked, forward_row)
        return result.reshape((kernel_count,) + image.shape).astype(jnp.bfloat16)

    rowblur = lax.map(blur_cell, latent)

    def one_exposure(total, inputs):
        coeffs, seen, cell, usable = inputs
        blurred = lax.dynamic_index_in_dim(rowblur, cell, 0, keepdims=False).astype(jnp.float32)
        vertical = jnp.swapaxes(filter_last(jnp.swapaxes(blurred, 1, 2), forward_col), 1, 2)
        predicted = jnp.sum(coeffs.astype(jnp.float32) * vertical, axis=0)
        residual = usable.astype(jnp.float32)[:, None] * (predicted - seen.astype(jnp.float32))
        weighted = lax.optimization_barrier((coeffs.astype(jnp.float32) * residual[None]).astype(jnp.bfloat16))
        colback = jnp.swapaxes(filter_last(jnp.swapaxes(weighted.astype(jnp.float32), 1, 2), adjoint_col), 1, 2)
        colback = lax.optimization_barrier(colback.astype(jnp.bfloat16))
        stacked = stacked_blocks(colback.astype(jnp.float32))
        own_term = jnp.einsum('kabp,kpq->abq', stacked, adjoint_row).reshape(residual.shape)
        selector = (jnp.arange(cell_count) == cell).astype(jnp.float32)
        total = total + selector[:, None, None] * own_term[None]
        return total, residual

    start = jnp.zeros(latent.shape, jnp.float32)
    gradient, residuals = lax.scan(one_exposure, start, (coefficients, observed, cell_of[:, 0].astype(jnp.int32), valid_rows))
    return gradient, residuals
```

```python
import functools

import jax
import jax.numpy as jnp
from jax import lax
from jax.experimental import pallas as pl
from jax.experimental.pallas import tpu as pltpu
from jax.sharding import PartitionSpec as P

LANES = 128
WINDOW = 256
PACK = 16
STEP = 64


def round_up(value, step):
    return -(-value // step) * step


def from_behind(block, axis, distance):
    devices = range(lax.axis_size(axis))
    route = [(i - distance, i) for i in devices if i - distance in devices]
    return lax.ppermute(block, axis, route)


def toeplitz(taps_row, rows, first):
    parts = []
    for at in range(0, rows, STEP):
        moved = pltpu.roll(jnp.broadcast_to(taps_row, (8, WINDOW)), (first + at) % WINDOW, 1)
        spread = jnp.broadcast_to(moved[:1], (min(STEP, rows - at), WINDOW))
        parts.append(pltpu.roll(spread, 0, 1, stride=1, stride_axis=0))
    return jnp.concatenate(parts, axis=0)


def filters_kernel(
    dims,
    lat_ref, taps_ref, obs_ref, mask_ref, coef_hbm, above_hbm, below_hbm,
    res_ref, term_ref,
    coef, lsh, fw, gw, aw, bw, rb, resid, cb, tsh, sems,
):
    kernels, tap_count, strip, width, inner, outer = dims
    half_width = tap_count // 2
    half = strip // 2
    block = half + inner
    chunks = width // WINDOW

    def copies(c):
        cols = pl.ds(c * WINDOW, WINDOW)
        return (
            pltpu.make_async_copy(
                coef_hbm.at[:, :, cols], coef.at[:, pl.ds(inner, strip), cols], sems.at[c, 0]),
            pltpu.make_async_copy(
                above_hbm.at[:, :, cols], coef.at[:, pl.ds(0, inner), cols], sems.at[c, 1]),
            pltpu.make_async_copy(
                below_hbm.at[:, :, cols], coef.at[:, pl.ds(inner + strip, inner), cols], sems.at[c, 2]),
        )

    for c in range(chunks):
        for copy in copies(c):
            copy.start()

    lsh[:, pl.ds(0, LANES)] = jnp.zeros((lsh.shape[0], LANES), lsh.dtype)
    lsh[:, pl.ds(width, LANES)] = jnp.zeros((lsh.shape[0], LANES), lsh.dtype)
    lsh[:, pl.ds(LANES // 2, width)] = lat_ref[...]

    low_a = strip + 2 * outer - WINDOW
    low_b = strip + 2 * inner - WINDOW
    side = LANES // 2 + half_width

    @pl.loop(0, kernels // 2)
    def _(pair):
        for odd in range(2):
            k = 2 * pair + odd
            row = taps_ref[0, pl.ds(k, 1), :]
            row_rev = taps_ref[1, pl.ds(k, 1), :]
            col = taps_ref[2, pl.ds(k, 1), :]
            col_rev = taps_ref[3, pl.ds(k, 1), :]
            shape = (pl.ds(odd * LANES, LANES))
            fw[pair, :, shape] = toeplitz(row_rev, WINDOW, -side)[:, :LANES].astype(fw.dtype)
            gw[k] = toeplitz(row, WINDOW, -side)[:, :LANES].astype(gw.dtype)
            aw[k, 0] = toeplitz(col, block, outer - inner - half_width).astype(aw.dtype)
            aw[k, 1] = toeplitz(col, block, half + outer - half_width - low_a).astype(aw.dtype)
            bw[k, 0] = toeplitz(col_rev, half, inner - half_width).astype(bw.dtype)
            bw[k, 1] = toeplitz(col_rev, half, half + inner - half_width - low_b).astype(bw.dtype)

    @pl.loop(0, chunks)
    def _(c):
        for copy in copies(c):
            copy.wait()
        start = pl.multiple_of(c * WINDOW, WINDOW)
        cols = pl.ds(start, WINDOW)
        for b in range(WINDOW // LANES):
            window = lsh[:, pl.ds(pl.multiple_of(start + b * LANES, LANES), WINDOW)]
            for pair in range(kernels // 2):
                both = jnp.dot(window, fw[pair], preferred_element_type=jnp.float32).astype(rb.dtype)
                rb[2 * pair, :, pl.ds(b * LANES, LANES)] = both[:, :LANES]
                rb[2 * pair + 1, :, pl.ds(b * LANES, LANES)] = both[:, LANES:]
        for part in range(2):
            rows = pl.ds(part * block, block)
            seen = pl.ds(part * low_a, WINDOW)
            predicted = jnp.zeros((block, WINDOW), jnp.float32)
            for k in range(kernels):
                vertical = jnp.dot(aw[k, part], rb[k, seen, :], preferred_element_type=jnp.float32)
                predicted += coef[k, rows, cols].astype(jnp.float32) * vertical
            mask = mask_ref[rows, :]
            mask = jnp.concatenate([mask] * (WINDOW // LANES), axis=1)
            resid[rows, :] = mask * (predicted - obs_ref[rows, cols].astype(jnp.float32))
        res_ref[:, cols] = resid[pl.ds(inner, strip), :]
        for k in range(kernels):
            weighted = (coef[k, :, cols].astype(jnp.float32) * resid[...]).astype(jnp.bfloat16)
            for part in range(2):
                seen = weighted[part * low_b:part * low_b + WINDOW]
                back = jnp.dot(bw[k, part], seen, preferred_element_type=jnp.float32)
                cb[k, pl.ds(part * half, half), cols] = back.astype(cb.dtype)

    blocks = width // LANES
    for out, source, taps_at in (
        (0, 0, LANES), (width, width - LANES, 0),
    ):
        total = jnp.zeros((strip, LANES), jnp.float32)
        for k in range(kernels):
            total += jnp.dot(
                cb[k, :, pl.ds(source, LANES)], gw[k, pl.ds(taps_at, LANES), :],
                preferred_element_type=jnp.float32)
        tsh[:, pl.ds(out, LANES)] = total

    @pl.loop(0, blocks - 1)
    def _(b):
        source = pl.multiple_of(b * LANES, LANES)
        total = jnp.zeros((strip, LANES), jnp.float32)
        for k in range(kernels):
            total += jnp.dot(
                cb[k, :, pl.ds(source, WINDOW)], gw[k], preferred_element_type=jnp.float32)
        tsh[:, pl.ds(pl.multiple_of(source + LANES, LANES), LANES)] = total

    term_ref[...] = tsh[:, pl.ds(LANES // 2, width)].astype(term_ref.dtype)


def body(latent, row_taps, column_taps, coefficients, observed, cell_of, valid_rows):
    kernels, tap_count = row_taps.shape
    half_width = tap_count // 2
    strip, width = observed.shape[1:]
    ncells = latent.shape[0]
    inner = round_up(half_width, PACK)
    outer = round_up(2 * half_width, PACK)
    cell_list = cell_of[:, 0]

    above_coef = from_behind(coefficients[0, :, strip - inner:], "row", 1)
    below_coef = from_behind(coefficients[0, :, :inner], "row", -1)
    usable = jnp.broadcast_to(valid_rows[0].astype(jnp.bfloat16)[:, None], (strip, LANES))
    seen = jnp.concatenate([observed[0], usable], axis=1)
    seen = jnp.concatenate(
        [from_behind(seen[strip - inner:], "row", 1), seen, from_behind(seen[:inner], "row", -1)], axis=0)
    mask = seen[:, width:].astype(jnp.float32)
    seen = seen[:, :width]

    outgoing = jnp.take(latent, cell_list, axis=0)
    arrived = lax.all_to_all(outgoing, "exp", split_axis=0, concat_axis=2, tiled=True)[0]
    extended = jnp.concatenate(
        [from_behind(arrived[strip - outer:], "row", 1), arrived, from_behind(arrived[:outer], "row", -1)], axis=0)

    taps = jnp.stack([row_taps, row_taps[:, ::-1], column_taps, column_taps[:, ::-1]]).astype(jnp.float32)
    taps = jnp.pad(taps, ((0, 0), (0, 0), (0, WINDOW - tap_count)))

    vmem = pl.BlockSpec(memory_space=pltpu.VMEM)
    hbm = pl.BlockSpec(memory_space=pl.ANY)
    dims = (kernels, tap_count, strip, width, inner, outer)
    block = strip // 2 + inner
    bf16 = jnp.bfloat16
    residual, term = pl.pallas_call(
        functools.partial(filters_kernel, dims),
        out_shape=(
            jax.ShapeDtypeStruct((strip, width), jnp.float32),
            jax.ShapeDtypeStruct((strip, width), bf16),
        ),
        in_specs=[vmem, vmem, vmem, vmem, hbm, hbm, hbm],
        out_specs=(vmem, vmem),
        scratch_shapes=[
            pltpu.VMEM((kernels, strip + 2 * inner, width), bf16),
            pltpu.VMEM((strip + 2 * outer, width + LANES), bf16),
            pltpu.VMEM((kernels // 2, WINDOW, 2 * LANES), bf16),
            pltpu.VMEM((kernels, WINDOW, LANES), bf16),
            pltpu.VMEM((kernels, 2, block, WINDOW), bf16),
            pltpu.VMEM((kernels, 2, strip // 2, WINDOW), bf16),
            pltpu.VMEM((kernels, strip + 2 * outer, WINDOW), bf16),
            pltpu.VMEM((strip + 2 * inner, WINDOW), jnp.float32),
            pltpu.VMEM((kernels, strip, width), bf16),
            pltpu.VMEM((strip, width + LANES), jnp.float32),
            pltpu.SemaphoreType.DMA((width // WINDOW, 3)),
        ],
        compiler_params=pltpu.CompilerParams(vmem_limit_bytes=56 * 2**20),
        cost_estimate=pl.CostEstimate(flops=10**10, bytes_accessed=2 * 10**7, transcendentals=0),
    )(extended, taps, seen, mask, coefficients[0], above_coef, below_coef)

    incoming = lax.all_to_all(term[None], "exp", split_axis=2, concat_axis=0, tiled=True)
    owner = jnp.arange(ncells)[:, None] == cell_list[None, :]
    gradient = jnp.sum(
        jnp.where(owner[:, :, None, None], incoming[None].astype(jnp.float32), 0.0), axis=1)
    return (gradient, residual[None])


def solution(mesh):
    placed = (
        P(None, "row", "exp"),
        P(),
        P(),
        P("exp", None, "row", None),
        P("exp", "row", None),
        P(),
        P("exp", "row"),
    )
    return jax.shard_map(
        body,
        mesh=mesh,
        in_specs=placed,
        out_specs=(P(None, "row", "exp"), P("exp", "row", None)),
        check_vma=False,
    )
```

```python
import functools

import jax
import jax.numpy as jnp
from jax import lax
from jax.experimental import pallas as pl
from jax.experimental.pallas import tpu as pltpu
from jax.sharding import PartitionSpec as P

LANES = 128
WINDOW = 256
PACK = 16
STEP = 64
MESH = pl.DeviceIdType.MESH


def round_up(value, step):
    return -(-value // step) * step


def from_behind(block, axis, distance):
    devices = range(lax.axis_size(axis))
    route = [(i - distance, i) for i in devices if i - distance in devices]
    return lax.ppermute(block, axis, route)


def toeplitz(taps_row, rows, first):
    parts = []
    for at in range(0, rows, STEP):
        moved = pltpu.roll(jnp.broadcast_to(taps_row, (8, WINDOW)), (first + at) % WINDOW, 1)
        spread = jnp.broadcast_to(moved[:1], (min(STEP, rows - at), WINDOW))
        parts.append(pltpu.roll(spread, 0, 1, stride=1, stride_axis=0))
    return jnp.concatenate(parts, axis=0)


def filters_kernel(
    dims,
    lat_ref, taps_ref, obs_ref, mask_ref, coef_hbm, above_hbm, below_hbm,
    res_ref, term_ref,
    coef, lsh, fw, gw, aw, bw, rb, resid, cb, tsh, sems,
):
    kernels, tap_count, strip, width, inner, outer = dims
    half_width = tap_count // 2
    half = strip // 2
    block = half + inner
    chunks = width // WINDOW

    def copies(c):
        cols = pl.ds(c * WINDOW, WINDOW)
        return (
            pltpu.make_async_copy(
                coef_hbm.at[:, :, cols], coef.at[:, pl.ds(inner, strip), cols], sems.at[c, 0]),
            pltpu.make_async_copy(
                above_hbm.at[:, :, cols], coef.at[:, pl.ds(0, inner), cols], sems.at[c, 1]),
            pltpu.make_async_copy(
                below_hbm.at[:, :, cols], coef.at[:, pl.ds(inner + strip, inner), cols], sems.at[c, 2]),
        )

    for c in range(chunks):
        for copy in copies(c):
            copy.start()

    lsh[:, pl.ds(0, LANES)] = jnp.zeros((lsh.shape[0], LANES), lsh.dtype)
    lsh[:, pl.ds(width, LANES)] = jnp.zeros((lsh.shape[0], LANES), lsh.dtype)
    lsh[:, pl.ds(LANES // 2, width)] = lat_ref[...]

    low_a = strip + 2 * outer - WINDOW
    low_b = strip + 2 * inner - WINDOW
    side = LANES // 2 + half_width

    @pl.loop(0, kernels // 2)
    def _(pair):
        for odd in range(2):
            k = 2 * pair + odd
            row = taps_ref[0, pl.ds(k, 1), :]
            row_rev = taps_ref[1, pl.ds(k, 1), :]
            col = taps_ref[2, pl.ds(k, 1), :]
            col_rev = taps_ref[3, pl.ds(k, 1), :]
            shape = (pl.ds(odd * LANES, LANES))
            fw[pair, :, shape] = toeplitz(row_rev, WINDOW, -side)[:, :LANES].astype(fw.dtype)
            gw[k] = toeplitz(row, WINDOW, -side)[:, :LANES].astype(gw.dtype)
            aw[k, 0] = toeplitz(col, block, outer - inner - half_width).astype(aw.dtype)
            aw[k, 1] = toeplitz(col, block, half + outer - half_width - low_a).astype(aw.dtype)
            bw[k, 0] = toeplitz(col_rev, half, inner - half_width).astype(bw.dtype)
            bw[k, 1] = toeplitz(col_rev, half, half + inner - half_width - low_b).astype(bw.dtype)

    @pl.loop(0, chunks)
    def _(c):
        for copy in copies(c):
            copy.wait()
        start = pl.multiple_of(c * WINDOW, WINDOW)
        cols = pl.ds(start, WINDOW)
        for b in range(WINDOW // LANES):
            window = lsh[:, pl.ds(pl.multiple_of(start + b * LANES, LANES), WINDOW)]
            for pair in range(kernels // 2):
                both = jnp.dot(window, fw[pair], preferred_element_type=jnp.float32).astype(rb.dtype)
                rb[2 * pair, :, pl.ds(b * LANES, LANES)] = both[:, :LANES]
                rb[2 * pair + 1, :, pl.ds(b * LANES, LANES)] = both[:, LANES:]
        for part in range(2):
            rows = pl.ds(part * block, block)
            seen = pl.ds(part * low_a, WINDOW)
            predicted = jnp.zeros((block, WINDOW), jnp.float32)
            for k in range(kernels):
                vertical = jnp.dot(aw[k, part], rb[k, seen, :], preferred_element_type=jnp.float32)
                predicted += coef[k, rows, cols].astype(jnp.float32) * vertical
            mask = mask_ref[rows, :]
            mask = jnp.concatenate([mask] * (WINDOW // LANES), axis=1)
            resid[rows, :] = mask * (predicted - obs_ref[rows, cols].astype(jnp.float32))
        res_ref[:, cols] = resid[pl.ds(inner, strip), :]
        for k in range(kernels):
            weighted = (coef[k, :, cols].astype(jnp.float32) * resid[...]).astype(jnp.bfloat16)
            for part in range(2):
                seen = weighted[part * low_b:part * low_b + WINDOW]
                back = jnp.dot(bw[k, part], seen, preferred_element_type=jnp.float32)
                cb[k, pl.ds(part * half, half), cols] = back.astype(cb.dtype)

    blocks = width // LANES
    for out, source, taps_at in (
        (0, 0, LANES), (width, width - LANES, 0),
    ):
        total = jnp.zeros((strip, LANES), jnp.float32)
        for k in range(kernels):
            total += jnp.dot(
                cb[k, :, pl.ds(source, LANES)], gw[k, pl.ds(taps_at, LANES), :],
                preferred_element_type=jnp.float32)
        tsh[:, pl.ds(out, LANES)] = total

    @pl.loop(0, blocks - 1)
    def _(b):
        source = pl.multiple_of(b * LANES, LANES)
        total = jnp.zeros((strip, LANES), jnp.float32)
        for k in range(kernels):
            total += jnp.dot(
                cb[k, :, pl.ds(source, WINDOW)], gw[k], preferred_element_type=jnp.float32)
        tsh[:, pl.ds(pl.multiple_of(source + LANES, LANES), LANES)] = total

    term_ref[...] = tsh[:, pl.ds(LANES // 2, width)].astype(term_ref.dtype)


def apart_body(latent, row_taps, column_taps, coefficients, observed, cell_of, valid_rows):
    kernels, tap_count = row_taps.shape
    half_width = tap_count // 2
    strip, width = observed.shape[1:]
    ncells = latent.shape[0]
    inner = round_up(half_width, PACK)
    outer = round_up(2 * half_width, PACK)
    cell_list = cell_of[:, 0]

    above_coef = from_behind(coefficients[0, :, strip - inner:], "row", 1)
    below_coef = from_behind(coefficients[0, :, :inner], "row", -1)
    usable = jnp.broadcast_to(valid_rows[0].astype(jnp.bfloat16)[:, None], (strip, LANES))
    seen = jnp.concatenate([observed[0], usable], axis=1)
    seen = jnp.concatenate(
        [from_behind(seen[strip - inner:], "row", 1), seen, from_behind(seen[:inner], "row", -1)], axis=0)
    mask = seen[:, width:].astype(jnp.float32)
    seen = seen[:, :width]

    outgoing = jnp.take(latent, cell_list, axis=0)
    arrived = lax.all_to_all(outgoing, "exp", split_axis=0, concat_axis=2, tiled=True)[0]
    extended = jnp.concatenate(
        [from_behind(arrived[strip - outer:], "row", 1), arrived, from_behind(arrived[:outer], "row", -1)], axis=0)

    taps = jnp.stack([row_taps, row_taps[:, ::-1], column_taps, column_taps[:, ::-1]]).astype(jnp.float32)
    taps = jnp.pad(taps, ((0, 0), (0, 0), (0, WINDOW - tap_count)))

    vmem = pl.BlockSpec(memory_space=pltpu.VMEM)
    hbm = pl.BlockSpec(memory_space=pl.ANY)
    dims = (kernels, tap_count, strip, width, inner, outer)
    block = strip // 2 + inner
    bf16 = jnp.bfloat16
    residual, term = pl.pallas_call(
        functools.partial(filters_kernel, dims),
        out_shape=(
            jax.ShapeDtypeStruct((strip, width), jnp.float32),
            jax.ShapeDtypeStruct((strip, width), bf16),
        ),
        in_specs=[vmem, vmem, vmem, vmem, hbm, hbm, hbm],
        out_specs=(vmem, vmem),
        scratch_shapes=[
            pltpu.VMEM((kernels, strip + 2 * inner, width), bf16),
            pltpu.VMEM((strip + 2 * outer, width + LANES), bf16),
            pltpu.VMEM((kernels // 2, WINDOW, 2 * LANES), bf16),
            pltpu.VMEM((kernels, WINDOW, LANES), bf16),
            pltpu.VMEM((kernels, 2, block, WINDOW), bf16),
            pltpu.VMEM((kernels, 2, strip // 2, WINDOW), bf16),
            pltpu.VMEM((kernels, strip + 2 * outer, WINDOW), bf16),
            pltpu.VMEM((strip + 2 * inner, WINDOW), jnp.float32),
            pltpu.VMEM((kernels, strip, width), bf16),
            pltpu.VMEM((strip, width + LANES), jnp.float32),
            pltpu.SemaphoreType.DMA((width // WINDOW, 3)),
        ],
        compiler_params=pltpu.CompilerParams(vmem_limit_bytes=56 * 2**20),
        cost_estimate=pl.CostEstimate(flops=10**10, bytes_accessed=2 * 10**7, transcendentals=0),
    )(extended, taps, seen, mask, coefficients[0], above_coef, below_coef)

    incoming = lax.all_to_all(term[None], "exp", split_axis=2, concat_axis=0, tiled=True)
    owner = jnp.arange(ncells)[:, None] == cell_list[None, :]
    gradient = jnp.sum(
        jnp.where(owner[:, :, None, None], incoming[None].astype(jnp.float32), 0.0), axis=1)
    return (gradient, residual[None])


def fused_kernel(
    dims,
    cells_ref, lat_ref, taps_ref, obs_hbm, use_hbm, coef_hbm,
    res_ref, grad_ref,
    coef, seen, usable, outgoing, lat, lsh, fw, gw, aw, bw, rb, resid, cb, tsh, leaving, arrived,
    own_sems, lat_send, lat_recv, rim_send, rim_recv, halo_send, halo_recv, term_send, term_recv,
):
    count, row_count, kernels, tap_count, strip, width, inner, outer = dims
    half_width = tap_count // 2
    half = strip // 2
    block = half + inner
    chunks = width // WINDOW
    per = WINDOW // LANES
    me = lax.axis_index("exp")
    row = lax.axis_index("row")
    rising = me < count // 2
    has_above = row > 0
    has_below = row < row_count - 1

    def ordered(rank, length):
        return jnp.where(rising, rank, length - 1 - rank)

    def reversed_order(rank, length):
        return jnp.where(rising, length - 1 - rank, rank)

    def lane_block(b):
        return pl.ds(pl.multiple_of(b * LANES, LANES), LANES)

    def chunk_cols(c):
        return pl.ds(pl.multiple_of(c * WINDOW, WINDOW), WINDOW)

    barrier = pltpu.get_barrier_semaphore()
    for e in range(count):
        @pl.when(e != me)
        def _():
            pl.semaphore_signal(barrier, inc=1, device_id={"exp": e}, device_id_type=MESH)

    @pl.when(has_above)
    def _():
        pl.semaphore_signal(barrier, inc=1, device_id={"row": row - 1}, device_id_type=MESH)

    @pl.when(has_below)
    def _():
        pl.semaphore_signal(barrier, inc=1, device_id={"row": row + 1}, device_id_type=MESH)

    def own_coef(c):
        cols = chunk_cols(c)
        return pltpu.make_async_copy(
            coef_hbm.at[:, :, cols], coef.at[:, pl.ds(inner, strip), cols], own_sems.at[c])

    own_seen = pltpu.make_async_copy(obs_hbm, seen.at[pl.ds(inner, strip)], own_sems.at[chunks])
    own_use = pltpu.make_async_copy(use_hbm, usable.at[pl.ds(inner, strip)], own_sems.at[chunks + 1])
    own_seen.start()
    own_use.start()
    for step in range(chunks):
        own_coef(ordered(step, chunks)).start()

    for e in range(count):
        outgoing[e] = lat_ref[cells_ref[e, 0]]
    for ref in (lat,):
        ref[:, pl.ds(0, LANES)] = jnp.zeros((ref.shape[0], LANES), ref.dtype)
        ref[:, pl.ds(LANES + width, LANES)] = jnp.zeros((ref.shape[0], LANES), ref.dtype)

    def fill(at_lat, at_inner):
        lat[pl.ds(at_lat, outer), :] = jnp.zeros((outer, lat.shape[1]), lat.dtype)
        coef[:, pl.ds(at_inner, inner), :] = jnp.zeros((kernels, inner, width), coef.dtype)
        seen[pl.ds(at_inner, inner), :] = jnp.zeros((inner, width), seen.dtype)
        usable[pl.ds(at_inner, inner), :] = jnp.zeros((inner, LANES), usable.dtype)

    @pl.when(jnp.logical_not(has_above))
    def _():
        fill(0, 0)

    @pl.when(jnp.logical_not(has_below))
    def _():
        fill(outer + strip, inner + strip)

    pl.semaphore_wait(barrier, count - 1 + has_above.astype(jnp.int32) + has_below.astype(jnp.int32))

    strip_rows = pl.ds(outer, strip)

    def lat_copy(e):
        return pltpu.make_async_remote_copy(
            src_ref=outgoing.at[e], dst_ref=lat.at[strip_rows, lane_block(me + 1)],
            send_sem=lat_send.at[e], recv_sem=lat_recv.at[me],
            device_id={"exp": e}, device_id_type=MESH)

    def own_lat():
        return pltpu.make_async_copy(
            outgoing.at[me], lat.at[strip_rows, lane_block(me + 1)], lat_recv.at[me])

    def halo_copies(c, side):
        cols = chunk_cols(c)
        source = pl.ds(0 if side == 0 else strip - inner, inner)
        target = pl.ds(inner + strip if side == 0 else 0, inner)
        return pltpu.make_async_remote_copy(
            src_ref=coef_hbm.at[:, source, cols], dst_ref=coef.at[:, target, cols],
            send_sem=halo_send.at[side, c], recv_sem=halo_recv.at[side, c],
            device_id={"row": row - 1 if side == 0 else row + 1}, device_id_type=MESH)

    def seen_copies(side):
        source = pl.ds(0 if side == 0 else strip - inner, inner)
        target = pl.ds(inner + strip if side == 0 else 0, inner)
        return [pltpu.make_async_remote_copy(
            src_ref=src.at[source], dst_ref=dst.at[target],
            send_sem=halo_send.at[side, chunks + i], recv_sem=halo_recv.at[side, chunks + i],
            device_id={"row": row - 1 if side == 0 else row + 1}, device_id_type=MESH)
            for i, (src, dst) in enumerate(((obs_hbm, seen), (use_hbm, usable)))]

    def rim_copy(b, side):
        cols = lane_block(b + 1)
        source = pl.ds(outer if side == 0 else strip, outer)
        target = pl.ds(outer + strip if side == 0 else 0, outer)
        return pltpu.make_async_remote_copy(
            src_ref=lat.at[source, cols], dst_ref=lat.at[target, cols],
            send_sem=rim_send.at[side, b], recv_sem=rim_recv.at[side, b],
            device_id={"row": row - 1 if side == 0 else row + 1}, device_id_type=MESH)

    sends = ((0, has_above), (1, has_below))
    receives = ((0, has_below), (1, has_above))

    own_lat().start()
    for rank in range(count):
        e = ordered(rank, count)
        @pl.when(e != me)
        def _():
            lat_copy(e).start()
    for side, there in sends:
        @pl.when(there)
        def _():
            for copy in seen_copies(side):
                copy.start()
            for step in range(chunks):
                halo_copies(ordered(step, chunks), side).start()

    low_a = strip + 2 * outer - WINDOW
    low_b = strip + 2 * inner - WINDOW
    shift = LANES // 2 + half_width

    @pl.loop(0, kernels // 2)
    def _(pair):
        for odd in range(2):
            k = 2 * pair + odd
            along = taps_ref[0, pl.ds(k, 1), :]
            along_rev = taps_ref[1, pl.ds(k, 1), :]
            down = taps_ref[2, pl.ds(k, 1), :]
            down_rev = taps_ref[3, pl.ds(k, 1), :]
            fw[pair, :, pl.ds(odd * LANES, LANES)] = toeplitz(along_rev, WINDOW, -shift)[:, :LANES].astype(fw.dtype)
            gw[k] = toeplitz(along, WINDOW, -shift)[:, :LANES].astype(gw.dtype)
            aw[k, 0] = toeplitz(down, block, outer - inner - half_width).astype(aw.dtype)
            aw[k, 1] = toeplitz(down, block, half + outer - half_width - low_a).astype(aw.dtype)
            bw[k, 0] = toeplitz(down_rev, half, inner - half_width).astype(bw.dtype)
            bw[k, 1] = toeplitz(down_rev, half, half + inner - half_width - low_b).astype(bw.dtype)

    for at in (0, LANES + width):
        cb[:, :, pl.ds(at, LANES)] = jnp.zeros((kernels, strip, LANES), cb.dtype)

    def take_block(rank):
        b = ordered(rank, count)
        pltpu.make_async_copy(
            outgoing.at[0], lat.at[strip_rows, lane_block(b + 1)], lat_recv.at[b]).wait()
        for side, there in sends:
            @pl.when(there)
            def _():
                rim_copy(b, side).start()

    def take_rims(rank):
        b = ordered(rank, count)
        for side, there in receives:
            @pl.when(there)
            def _():
                rim_copy(b, side).wait_recv()

    for rank in range(per + 1):
        take_block(rank)
    own_seen.wait()
    own_use.wait()
    for side, there in receives:
        @pl.when(there)
        def _():
            for copy in seen_copies(side):
                copy.wait_recv()
    take_rims(0)

    @pl.loop(0, chunks)
    def _(step):
        c = ordered(step, chunks)
        cols = chunk_cols(c)
        for more in range(1, per + 1):
            @pl.when(step * per + more < count)
            def _():
                take_rims(step * per + more)
        near = lat[:, pl.ds(pl.multiple_of(c * WINDOW, WINDOW), WINDOW + 2 * LANES)]
        lsh[...] = near[:, LANES // 2:LANES // 2 + WINDOW + LANES]
        for b in range(per):
            window = lsh[:, pl.ds(b * LANES, WINDOW)]
            for pair in range(kernels // 2):
                both = jnp.dot(window, fw[pair], preferred_element_type=jnp.float32).astype(rb.dtype)
                rb[2 * pair, :, pl.ds(b * LANES, LANES)] = both[:, :LANES]
                rb[2 * pair + 1, :, pl.ds(b * LANES, LANES)] = both[:, LANES:]
        own_coef(c).wait()
        for side, there in receives:
            @pl.when(there)
            def _():
                halo_copies(c, side).wait_recv()
        for part in range(2):
            if part == 1:
                for more in range(1, per + 1):
                    @pl.when((step + 1) * per + more < count)
                    def _():
                        take_block((step + 1) * per + more)
            rows = pl.ds(part * block, block)
            reach = pl.ds(part * low_a, WINDOW)
            predicted = jnp.zeros((block, WINDOW), jnp.float32)
            for k in range(kernels):
                vertical = jnp.dot(aw[k, part], rb[k, reach, :], preferred_element_type=jnp.float32)
                predicted += coef[k, rows, cols].astype(jnp.float32) * vertical
            mask = usable[rows, :].astype(jnp.float32)
            mask = jnp.concatenate([mask] * per, axis=1)
            resid[rows, cols] = mask * (predicted - seen[rows, cols].astype(jnp.float32))
        res_ref[:, cols] = resid[pl.ds(inner, strip), cols]

    def term_copy(b):
        return pltpu.make_async_remote_copy(
            src_ref=leaving.at[b], dst_ref=arrived.at[me],
            send_sem=term_send.at[b], recv_sem=term_recv.at[me],
            device_id={"exp": b}, device_id_type=MESH)

    def window_sum(rank):
        m = reversed_order(rank, count + 1)
        reach = pl.ds(pl.multiple_of(m * LANES, LANES), WINDOW)
        total = jnp.zeros((strip, LANES), jnp.float32)
        for k in range(kernels):
            total += jnp.dot(cb[k, :, reach], gw[k], preferred_element_type=jnp.float32)
        tsh[:, lane_block(m)] = total

    def send_term(rank):
        b = reversed_order(rank, count)
        both = tsh[:, pl.ds(pl.multiple_of(b * LANES, LANES), WINDOW)]
        leaving[b] = both[:, LANES // 2:LANES // 2 + LANES].astype(leaving.dtype)

        @pl.when(b != me)
        def _():
            term_copy(b).start()

    @pl.loop(0, chunks)
    def _(step):
        c = reversed_order(step, chunks)
        cols = chunk_cols(c)
        ahead = pl.ds(pl.multiple_of(c * WINDOW + LANES, LANES), WINDOW)
        for k in range(kernels):
            weighted = (coef[k, :, cols].astype(jnp.float32) * resid[:, cols]).astype(jnp.bfloat16)
            for part in range(2):
                reach = weighted[part * low_b:part * low_b + WINDOW]
                back = jnp.dot(bw[k, part], reach, preferred_element_type=jnp.float32)
                cb[k, pl.ds(part * half, half), ahead] = back.astype(cb.dtype)

        @pl.loop(step * per, step * per + per)
        def _(rank):
            window_sum(rank)

            @pl.when(rank > 0)
            def _():
                send_term(rank - 1)

    window_sum(count)
    send_term(count - 1)

    for c in range(grad_ref.shape[0]):
        mine = (cells_ref[me, 0] == c).astype(jnp.float32)
        grad_ref[c] = mine * leaving[me].astype(jnp.float32)
    for rank in range(count):
        e = reversed_order(rank, count)

        @pl.when(e != me)
        def _():
            pltpu.make_async_copy(leaving.at[0], arrived.at[e], term_recv.at[e]).wait()
            value = arrived[e].astype(jnp.float32)
            for c in range(grad_ref.shape[0]):
                grad_ref[c] += (cells_ref[e, 0] == c).astype(jnp.float32) * value

    for e in range(count):
        @pl.when(e != me)
        def _():
            lat_copy(e).wait_send()
            term_copy(e).wait_send()
    for side, there in sends:
        @pl.when(there)
        def _():
            for copy in seen_copies(side):
                copy.wait_send()
            for c in range(chunks):
                halo_copies(c, side).wait_send()
            for b in range(count):
                rim_copy(b, side).wait_send()


def fused_body(latent, row_taps, column_taps, coefficients, observed, cell_of, valid_rows):
    kernels, tap_count = row_taps.shape
    half_width = tap_count // 2
    strip, width = observed.shape[1:]
    ncells = latent.shape[0]
    inner = round_up(half_width, PACK)
    outer = round_up(2 * half_width, PACK)
    count, row_count = lax.axis_size("exp"), lax.axis_size("row")
    usable = jnp.broadcast_to(valid_rows[0].astype(jnp.bfloat16)[:, None], (strip, LANES))
    taps = jnp.stack([row_taps, row_taps[:, ::-1], column_taps, column_taps[:, ::-1]]).astype(jnp.float32)
    taps = jnp.pad(taps, ((0, 0), (0, 0), (0, WINDOW - tap_count)))

    vmem = pl.BlockSpec(memory_space=pltpu.VMEM)
    smem = pl.BlockSpec(memory_space=pltpu.SMEM)
    hbm = pl.BlockSpec(memory_space=pl.ANY)
    chunks = width // WINDOW
    block = strip // 2 + inner
    bf16 = jnp.bfloat16
    dma = pltpu.SemaphoreType.DMA
    dims = (count, row_count, kernels, tap_count, strip, width, inner, outer)
    residual, gradient = pl.pallas_call(
        functools.partial(fused_kernel, dims),
        out_shape=(
            jax.ShapeDtypeStruct((strip, width), jnp.float32),
            jax.ShapeDtypeStruct((ncells, strip, LANES), jnp.float32),
        ),
        in_specs=[smem, vmem, vmem, hbm, hbm, hbm],
        out_specs=(vmem, vmem),
        scratch_shapes=[
            pltpu.VMEM((kernels, strip + 2 * inner, width), bf16),
            pltpu.VMEM((strip + 2 * inner, width), bf16),
            pltpu.VMEM((strip + 2 * inner, LANES), bf16),
            pltpu.VMEM((count, strip, LANES), bf16),
            pltpu.VMEM((strip + 2 * outer, width + 2 * LANES), bf16),
            pltpu.VMEM((strip + 2 * outer, WINDOW + LANES), bf16),
            pltpu.VMEM((kernels // 2, WINDOW, 2 * LANES), bf16),
            pltpu.VMEM((kernels, WINDOW, LANES), bf16),
            pltpu.VMEM((kernels, 2, block, WINDOW), bf16),
            pltpu.VMEM((kernels, 2, strip // 2, WINDOW), bf16),
            pltpu.VMEM((kernels, strip + 2 * outer, WINDOW), bf16),
            pltpu.VMEM((strip + 2 * inner, width), jnp.float32),
            pltpu.VMEM((kernels, strip, width + 2 * LANES), bf16),
            pltpu.VMEM((strip, width + LANES), jnp.float32),
            pltpu.VMEM((count, strip, LANES), bf16),
            pltpu.VMEM((count, strip, LANES), bf16),
            dma((chunks + 2,)),
            dma((count,)), dma((count,)),
            dma((2, count)), dma((2, count)),
            dma((2, chunks + 2)), dma((2, chunks + 2)),
            dma((count,)), dma((count,)),
        ],
        compiler_params=pltpu.CompilerParams(
            vmem_limit_bytes=56 * 2**20, collective_id=0, has_side_effects=True),
        cost_estimate=pl.CostEstimate(flops=10**10, bytes_accessed=2 * 10**7, transcendentals=0),
    )(cell_of, latent, taps, observed[0], usable, coefficients[0])
    return (gradient, residual[None])


def body(latent, *others):
    if latent.shape[2] == LANES:
        return fused_body(latent, *others)
    return apart_body(latent, *others)


def solution(mesh):
    placed = (
        P(None, "row", "exp"),
        P(),
        P(),
        P("exp", None, "row", None),
        P("exp", "row", None),
        P(),
        P("exp", "row"),
    )
    return jax.shard_map(
        body,
        mesh=mesh,
        in_specs=placed,
        out_specs=(P(None, "row", "exp"), P("exp", "row", None)),
        check_vma=False,
    )
```

```python
import functools

import jax
import jax.numpy as jnp
from jax import lax
from jax.experimental import pallas as pl
from jax.experimental.pallas import tpu as pltpu
from jax.sharding import PartitionSpec as P

LANES = 128
WINDOW = 256
PACK = 16
STEP = 64
MESH = pl.DeviceIdType.MESH


def round_up(value, step):
    return -(-value // step) * step


def from_behind(block, axis, distance):
    devices = range(lax.axis_size(axis))
    route = [(i - distance, i) for i in devices if i - distance in devices]
    return lax.ppermute(block, axis, route)


def toeplitz(taps_row, rows, first):
    parts = []
    for at in range(0, rows, STEP):
        moved = pltpu.roll(jnp.broadcast_to(taps_row, (8, WINDOW)), (first + at) % WINDOW, 1)
        spread = jnp.broadcast_to(moved[:1], (min(STEP, rows - at), WINDOW))
        parts.append(pltpu.roll(spread, 0, 1, stride=1, stride_axis=0))
    return jnp.concatenate(parts, axis=0)


def filters_kernel(
    dims,
    lat_ref, taps_ref, obs_ref, mask_ref, coef_hbm, above_hbm, below_hbm,
    res_ref, term_ref,
    coef, lsh, fw, gw, aw, bw, rb, resid, cb, tsh, sems,
):
    kernels, tap_count, strip, width, inner, outer = dims
    half_width = tap_count // 2
    half = strip // 2
    block = half + inner
    chunks = width // WINDOW

    def copies(c):
        cols = pl.ds(c * WINDOW, WINDOW)
        return (
            pltpu.make_async_copy(
                coef_hbm.at[:, :, cols], coef.at[:, pl.ds(inner, strip), cols], sems.at[c, 0]),
            pltpu.make_async_copy(
                above_hbm.at[:, :, cols], coef.at[:, pl.ds(0, inner), cols], sems.at[c, 1]),
            pltpu.make_async_copy(
                below_hbm.at[:, :, cols], coef.at[:, pl.ds(inner + strip, inner), cols], sems.at[c, 2]),
        )

    for c in range(chunks):
        for copy in copies(c):
            copy.start()

    lsh[:, pl.ds(0, LANES)] = jnp.zeros((lsh.shape[0], LANES), lsh.dtype)
    lsh[:, pl.ds(width, LANES)] = jnp.zeros((lsh.shape[0], LANES), lsh.dtype)
    lsh[:, pl.ds(LANES // 2, width)] = lat_ref[...]

    low_a = strip + 2 * outer - WINDOW
    low_b = strip + 2 * inner - WINDOW
    side = LANES // 2 + half_width

    @pl.loop(0, kernels // 2)
    def _(pair):
        for odd in range(2):
            k = 2 * pair + odd
            row = taps_ref[0, pl.ds(k, 1), :]
            row_rev = taps_ref[1, pl.ds(k, 1), :]
            col = taps_ref[2, pl.ds(k, 1), :]
            col_rev = taps_ref[3, pl.ds(k, 1), :]
            shape = (pl.ds(odd * LANES, LANES))
            fw[pair, :, shape] = toeplitz(row_rev, WINDOW, -side)[:, :LANES].astype(fw.dtype)
            gw[k] = toeplitz(row, WINDOW, -side)[:, :LANES].astype(gw.dtype)
            aw[k, 0] = toeplitz(col, block, outer - inner - half_width).astype(aw.dtype)
            aw[k, 1] = toeplitz(col, block, half + outer - half_width - low_a).astype(aw.dtype)
            bw[k, 0] = toeplitz(col_rev, half, inner - half_width).astype(bw.dtype)
            bw[k, 1] = toeplitz(col_rev, half, half + inner - half_width - low_b).astype(bw.dtype)

    @pl.loop(0, chunks)
    def _(c):
        for copy in copies(c):
            copy.wait()
        start = pl.multiple_of(c * WINDOW, WINDOW)
        cols = pl.ds(start, WINDOW)
        for b in range(WINDOW // LANES):
            window = lsh[:, pl.ds(pl.multiple_of(start + b * LANES, LANES), WINDOW)]
            for pair in range(kernels // 2):
                both = jnp.dot(window, fw[pair], preferred_element_type=jnp.float32).astype(rb.dtype)
                rb[2 * pair, :, pl.ds(b * LANES, LANES)] = both[:, :LANES]
                rb[2 * pair + 1, :, pl.ds(b * LANES, LANES)] = both[:, LANES:]
        for part in range(2):
            rows = pl.ds(part * block, block)
            seen = pl.ds(part * low_a, WINDOW)
            predicted = jnp.zeros((block, WINDOW), jnp.float32)
            for k in range(kernels):
                vertical = jnp.dot(aw[k, part], rb[k, seen, :], preferred_element_type=jnp.float32)
                predicted += coef[k, rows, cols].astype(jnp.float32) * vertical
            mask = mask_ref[rows, :]
            mask = jnp.concatenate([mask] * (WINDOW // LANES), axis=1)
            resid[rows, :] = mask * (predicted - obs_ref[rows, cols].astype(jnp.float32))
        res_ref[:, cols] = resid[pl.ds(inner, strip), :]
        for k in range(kernels):
            weighted = (coef[k, :, cols].astype(jnp.float32) * resid[...]).astype(jnp.bfloat16)
            for part in range(2):
                seen = weighted[part * low_b:part * low_b + WINDOW]
                back = jnp.dot(bw[k, part], seen, preferred_element_type=jnp.float32)
                cb[k, pl.ds(part * half, half), cols] = back.astype(cb.dtype)

    blocks = width // LANES
    for out, source, taps_at in (
        (0, 0, LANES), (width, width - LANES, 0),
    ):
        total = jnp.zeros((strip, LANES), jnp.float32)
        for k in range(kernels):
            total += jnp.dot(
                cb[k, :, pl.ds(source, LANES)], gw[k, pl.ds(taps_at, LANES), :],
                preferred_element_type=jnp.float32)
        tsh[:, pl.ds(out, LANES)] = total

    @pl.loop(0, blocks - 1)
    def _(b):
        source = pl.multiple_of(b * LANES, LANES)
        total = jnp.zeros((strip, LANES), jnp.float32)
        for k in range(kernels):
            total += jnp.dot(
                cb[k, :, pl.ds(source, WINDOW)], gw[k], preferred_element_type=jnp.float32)
        tsh[:, pl.ds(pl.multiple_of(source + LANES, LANES), LANES)] = total

    term_ref[...] = tsh[:, pl.ds(LANES // 2, width)].astype(term_ref.dtype)


def apart_body(latent, row_taps, column_taps, coefficients, observed, cell_of, valid_rows):
    kernels, tap_count = row_taps.shape
    half_width = tap_count // 2
    strip, width = observed.shape[1:]
    ncells = latent.shape[0]
    inner = round_up(half_width, PACK)
    outer = round_up(2 * half_width, PACK)
    cell_list = cell_of[:, 0]

    above_coef = from_behind(coefficients[0, :, strip - inner:], "row", 1)
    below_coef = from_behind(coefficients[0, :, :inner], "row", -1)
    usable = jnp.broadcast_to(valid_rows[0].astype(jnp.bfloat16)[:, None], (strip, LANES))
    seen = jnp.concatenate([observed[0], usable], axis=1)
    seen = jnp.concatenate(
        [from_behind(seen[strip - inner:], "row", 1), seen, from_behind(seen[:inner], "row", -1)], axis=0)
    mask = seen[:, width:].astype(jnp.float32)
    seen = seen[:, :width]

    outgoing = jnp.take(latent, cell_list, axis=0)
    arrived = lax.all_to_all(outgoing, "exp", split_axis=0, concat_axis=2, tiled=True)[0]
    extended = jnp.concatenate(
        [from_behind(arrived[strip - outer:], "row", 1), arrived, from_behind(arrived[:outer], "row", -1)], axis=0)

    taps = jnp.stack([row_taps, row_taps[:, ::-1], column_taps, column_taps[:, ::-1]]).astype(jnp.float32)
    taps = jnp.pad(taps, ((0, 0), (0, 0), (0, WINDOW - tap_count)))

    vmem = pl.BlockSpec(memory_space=pltpu.VMEM)
    hbm = pl.BlockSpec(memory_space=pl.ANY)
    dims = (kernels, tap_count, strip, width, inner, outer)
    block = strip // 2 + inner
    bf16 = jnp.bfloat16
    residual, term = pl.pallas_call(
        functools.partial(filters_kernel, dims),
        out_shape=(
            jax.ShapeDtypeStruct((strip, width), jnp.float32),
            jax.ShapeDtypeStruct((strip, width), bf16),
        ),
        in_specs=[vmem, vmem, vmem, vmem, hbm, hbm, hbm],
        out_specs=(vmem, vmem),
        scratch_shapes=[
            pltpu.VMEM((kernels, strip + 2 * inner, width), bf16),
            pltpu.VMEM((strip + 2 * outer, width + LANES), bf16),
            pltpu.VMEM((kernels // 2, WINDOW, 2 * LANES), bf16),
            pltpu.VMEM((kernels, WINDOW, LANES), bf16),
            pltpu.VMEM((kernels, 2, block, WINDOW), bf16),
            pltpu.VMEM((kernels, 2, strip // 2, WINDOW), bf16),
            pltpu.VMEM((kernels, strip + 2 * outer, WINDOW), bf16),
            pltpu.VMEM((strip + 2 * inner, WINDOW), jnp.float32),
            pltpu.VMEM((kernels, strip, width), bf16),
            pltpu.VMEM((strip, width + LANES), jnp.float32),
            pltpu.SemaphoreType.DMA((width // WINDOW, 3)),
        ],
        compiler_params=pltpu.CompilerParams(vmem_limit_bytes=56 * 2**20),
        cost_estimate=pl.CostEstimate(flops=10**10, bytes_accessed=2 * 10**7, transcendentals=0),
    )(extended, taps, seen, mask, coefficients[0], above_coef, below_coef)

    incoming = lax.all_to_all(term[None], "exp", split_axis=2, concat_axis=0, tiled=True)
    owner = jnp.arange(ncells)[:, None] == cell_list[None, :]
    gradient = jnp.sum(
        jnp.where(owner[:, :, None, None], incoming[None].astype(jnp.float32), 0.0), axis=1)
    return (gradient, residual[None])


def fused_kernel(
    dims,
    cells_ref, lat_ref, along_ref, down_ref, valid_ref, obs_hbm, coef_hbm,
    res_ref, grad_ref,
    cells, taps_ref, coef, seen, usable, outgoing, lat, lsh, fw, gw, aw, bw, rb, resid, cb, tsh, leaving, arrived,
    own_sems, lat_send, lat_recv, rim_send, rim_recv, halo_send, halo_recv, term_send, term_recv,
):
    count, row_count, kernels, tap_count, strip, width, inner, outer = dims
    half_width = tap_count // 2
    half = strip // 2
    block = half + inner
    chunks = width // WINDOW
    per = WINDOW // LANES
    me = lax.axis_index("exp")
    row = lax.axis_index("row")
    rising = me < count // 2
    has_above = row > 0
    has_below = row < row_count - 1

    def ordered(rank, length):
        return jnp.where(rising, rank, length - 1 - rank)

    def reversed_order(rank, length):
        return jnp.where(rising, length - 1 - rank, rank)

    def lane_block(b):
        return pl.ds(pl.multiple_of(b * LANES, LANES), LANES)

    def chunk_cols(c):
        return pl.ds(pl.multiple_of(c * WINDOW, WINDOW), WINDOW)

    barrier = pltpu.get_barrier_semaphore()
    for e in range(count):
        @pl.when(e != me)
        def _():
            pl.semaphore_signal(barrier, inc=1, device_id={"exp": e}, device_id_type=MESH)

    @pl.when(has_above)
    def _():
        pl.semaphore_signal(barrier, inc=1, device_id={"row": row - 1}, device_id_type=MESH)

    @pl.when(has_below)
    def _():
        pl.semaphore_signal(barrier, inc=1, device_id={"row": row + 1}, device_id_type=MESH)

    def own_coef(c):
        cols = chunk_cols(c)
        return pltpu.make_async_copy(
            coef_hbm.at[:, :, cols], coef.at[:, pl.ds(inner, strip), cols], own_sems.at[c])

    own_seen = pltpu.make_async_copy(obs_hbm, seen.at[pl.ds(inner, strip)], own_sems.at[chunks])
    own_seen.start()
    for step in range(chunks):
        own_coef(ordered(step, chunks)).start()

    for e in range(count):
        cells[e] = jnp.broadcast_to(cells_ref[:, e:e + 1], (8, LANES))

    def owned(e, c):
        return jnp.concatenate([(cells[e] == c).astype(jnp.float32)] * (strip // 8), axis=0) > 0.5

    for e in range(count):
        chosen = lat_ref[0].astype(jnp.float32)
        for c in range(1, lat_ref.shape[0]):
            chosen = jnp.where(owned(e, c), lat_ref[c].astype(jnp.float32), chosen)
        outgoing[e] = chosen.astype(outgoing.dtype)
    at_row = lax.broadcasted_iota(jnp.int32, (strip, strip), 0)
    at_col = lax.broadcasted_iota(jnp.int32, (strip, strip), 1)
    spread = jnp.where(at_row == at_col, valid_ref[...], 0).astype(jnp.bfloat16)
    usable[pl.ds(inner, strip), :] = jnp.dot(
        spread, jnp.ones((strip, LANES), jnp.bfloat16),
        preferred_element_type=jnp.float32).astype(usable.dtype)
    for ref in (lat,):
        ref[:, pl.ds(0, LANES)] = jnp.zeros((ref.shape[0], LANES), ref.dtype)
        ref[:, pl.ds(LANES + width, LANES)] = jnp.zeros((ref.shape[0], LANES), ref.dtype)

    def fill(at_lat, at_inner):
        lat[pl.ds(at_lat, outer), :] = jnp.zeros((outer, lat.shape[1]), lat.dtype)
        coef[:, pl.ds(at_inner, inner), :] = jnp.zeros((kernels, inner, width), coef.dtype)
        seen[pl.ds(at_inner, inner), :] = jnp.zeros((inner, width), seen.dtype)
        usable[pl.ds(at_inner, inner), :] = jnp.zeros((inner, LANES), usable.dtype)

    @pl.when(jnp.logical_not(has_above))
    def _():
        fill(0, 0)

    @pl.when(jnp.logical_not(has_below))
    def _():
        fill(outer + strip, inner + strip)

    pl.semaphore_wait(barrier, count - 1 + has_above.astype(jnp.int32) + has_below.astype(jnp.int32))

    strip_rows = pl.ds(outer, strip)

    def lat_copy(e):
        return pltpu.make_async_remote_copy(
            src_ref=outgoing.at[e], dst_ref=lat.at[strip_rows, lane_block(me + 1)],
            send_sem=lat_send.at[e], recv_sem=lat_recv.at[me],
            device_id={"exp": e}, device_id_type=MESH)

    def own_lat():
        return pltpu.make_async_copy(
            outgoing.at[me], lat.at[strip_rows, lane_block(me + 1)], lat_recv.at[me])

    def halo_copies(c, side):
        cols = chunk_cols(c)
        source = pl.ds(0 if side == 0 else strip - inner, inner)
        target = pl.ds(inner + strip if side == 0 else 0, inner)
        return pltpu.make_async_remote_copy(
            src_ref=coef_hbm.at[:, source, cols], dst_ref=coef.at[:, target, cols],
            send_sem=halo_send.at[side, c], recv_sem=halo_recv.at[side, c],
            device_id={"row": row - 1 if side == 0 else row + 1}, device_id_type=MESH)

    def seen_copies(side):
        source = 0 if side == 0 else strip - inner
        target = pl.ds(inner + strip if side == 0 else 0, inner)
        return [pltpu.make_async_remote_copy(
            src_ref=src.at[pl.ds(first + source, inner)], dst_ref=dst.at[target],
            send_sem=halo_send.at[side, chunks + i], recv_sem=halo_recv.at[side, chunks + i],
            device_id={"row": row - 1 if side == 0 else row + 1}, device_id_type=MESH)
            for i, (src, first, dst) in enumerate(((obs_hbm, 0, seen), (usable, inner, usable)))]

    def rim_copy(b, side):
        cols = lane_block(b + 1)
        source = pl.ds(outer if side == 0 else strip, outer)
        target = pl.ds(outer + strip if side == 0 else 0, outer)
        return pltpu.make_async_remote_copy(
            src_ref=lat.at[source, cols], dst_ref=lat.at[target, cols],
            send_sem=rim_send.at[side, b], recv_sem=rim_recv.at[side, b],
            device_id={"row": row - 1 if side == 0 else row + 1}, device_id_type=MESH)

    sends = ((0, has_above), (1, has_below))
    receives = ((0, has_below), (1, has_above))

    def start_halos(step):
        for side, there in sends:
            @pl.when(there)
            def _():
                halo_copies(ordered(step, chunks), side).start()

    late = ordered(me, count) < count // 4
    own_lat().start()
    for rank in range(count):
        e = ordered(rank, count)
        @pl.when(jnp.logical_and(e != me, jnp.logical_or(jnp.logical_not(late), rank < count // 2)))
        def _():
            lat_copy(e).start()
    start_halos(0)
    for side, there in sends:
        @pl.when(there)
        def _():
            for copy in seen_copies(side):
                copy.start()

    low_a = strip + 2 * outer - WINDOW
    low_b = strip + 2 * inner - WINDOW
    shift = LANES // 2 + half_width

    at_tap = lax.broadcasted_iota(jnp.int32, (tap_count, WINDOW), 0)
    at_lane = lax.broadcasted_iota(jnp.int32, (tap_count, WINDOW), 1)
    keep = (at_tap == at_lane).astype(jnp.float32).astype(jnp.bfloat16)
    turn = (at_tap + at_lane == tap_count - 1).astype(jnp.float32).astype(jnp.bfloat16)
    for i, (taps, order) in enumerate(((along_ref, keep), (along_ref, turn), (down_ref, keep), (down_ref, turn))):
        taps_ref[i] = jnp.dot(taps[...], order, preferred_element_type=jnp.float32)

    @pl.loop(0, kernels // 2)
    def _(pair):
        for odd in range(2):
            k = 2 * pair + odd
            along = taps_ref[0, pl.ds(k, 1), :]
            along_rev = taps_ref[1, pl.ds(k, 1), :]
            down = taps_ref[2, pl.ds(k, 1), :]
            down_rev = taps_ref[3, pl.ds(k, 1), :]
            fw[pair, :, pl.ds(odd * LANES, LANES)] = toeplitz(along_rev, WINDOW, -shift)[:, :LANES].astype(fw.dtype)
            gw[k] = toeplitz(along, WINDOW, -shift)[:, :LANES].astype(gw.dtype)
            aw[k, 0] = toeplitz(down, block, outer - inner - half_width).astype(aw.dtype)
            aw[k, 1] = toeplitz(down, block, half + outer - half_width - low_a).astype(aw.dtype)
            bw[k, 0] = toeplitz(down_rev, half, inner - half_width).astype(bw.dtype)
            bw[k, 1] = toeplitz(down_rev, half, half + inner - half_width - low_b).astype(bw.dtype)

    for at in (0, LANES + width):
        cb[:, :, pl.ds(at, LANES)] = jnp.zeros((kernels, strip, LANES), cb.dtype)

    def take_block(rank):
        b = ordered(rank, count)
        pltpu.make_async_copy(
            outgoing.at[0], lat.at[strip_rows, lane_block(b + 1)], lat_recv.at[b]).wait()
        for side, there in sends:
            @pl.when(there)
            def _():
                rim_copy(b, side).start()

    def take_rims(rank):
        b = ordered(rank, count)
        for side, there in receives:
            @pl.when(there)
            def _():
                rim_copy(b, side).wait_recv()

    for rank in range(count // 2, count):
        @pl.when(late)
        def _():
            lat_copy(ordered(rank, count)).start()
    for rank in range(per + 1):
        take_block(rank)
    own_seen.wait()
    for side, there in receives:
        @pl.when(there)
        def _():
            for copy in seen_copies(side):
                copy.wait_recv()
    take_rims(0)

    @pl.loop(0, chunks)
    def _(step):
        c = ordered(step, chunks)
        cols = chunk_cols(c)

        @pl.when(step + 1 < chunks)
        def _():
            start_halos(step + 1)

        for more in range(1, per + 1):
            @pl.when(step * per + more < count)
            def _():
                take_rims(step * per + more)
        near = lat[:, pl.ds(pl.multiple_of(c * WINDOW, WINDOW), WINDOW + 2 * LANES)]
        lsh[...] = near[:, LANES // 2:LANES // 2 + WINDOW + LANES]
        for b in range(per):
            window = lsh[:, pl.ds(b * LANES, WINDOW)]
            for pair in range(kernels // 2):
                both = jnp.dot(window, fw[pair], preferred_element_type=jnp.float32).astype(rb.dtype)
                rb[2 * pair, :, pl.ds(b * LANES, LANES)] = both[:, :LANES]
                rb[2 * pair + 1, :, pl.ds(b * LANES, LANES)] = both[:, LANES:]
        own_coef(c).wait()
        for side, there in receives:
            @pl.when(there)
            def _():
                halo_copies(c, side).wait_recv()
        for part in range(2):
            if part == 1:
                for more in range(1, per + 1):
                    @pl.when((step + 1) * per + more < count)
                    def _():
                        take_block((step + 1) * per + more)
            rows = pl.ds(part * block, block)
            reach = pl.ds(part * low_a, WINDOW)
            predicted = jnp.zeros((block, WINDOW), jnp.float32)
            for k in range(kernels):
                vertical = jnp.dot(aw[k, part], rb[k, reach, :], preferred_element_type=jnp.float32)
                predicted += coef[k, rows, cols].astype(jnp.float32) * vertical
            mask = usable[rows, :].astype(jnp.float32)
            mask = jnp.concatenate([mask] * per, axis=1)
            resid[rows, cols] = mask * (predicted - seen[rows, cols].astype(jnp.float32))
        res_ref[:, cols] = resid[pl.ds(inner, strip), cols]

    def term_copy(b):
        return pltpu.make_async_remote_copy(
            src_ref=leaving.at[b], dst_ref=arrived.at[me],
            send_sem=term_send.at[b], recv_sem=term_recv.at[me],
            device_id={"exp": b}, device_id_type=MESH)

    def window_sum(rank):
        m = reversed_order(rank, count + 1)
        reach = pl.ds(pl.multiple_of(m * LANES, LANES), WINDOW)
        total = jnp.zeros((strip, LANES), jnp.float32)
        for k in range(kernels):
            total += jnp.dot(cb[k, :, reach], gw[k], preferred_element_type=jnp.float32)
        tsh[:, lane_block(m)] = total

    def send_term(rank):
        b = reversed_order(rank, count)
        both = tsh[:, pl.ds(pl.multiple_of(b * LANES, LANES), WINDOW)]
        leaving[b] = both[:, LANES // 2:LANES // 2 + LANES].astype(leaving.dtype)

        @pl.when(b != me)
        def _():
            term_copy(b).start()

    @pl.loop(0, chunks)
    def _(step):
        c = reversed_order(step, chunks)
        cols = chunk_cols(c)
        ahead = pl.ds(pl.multiple_of(c * WINDOW + LANES, LANES), WINDOW)
        for k in range(kernels):
            weighted = (coef[k, :, cols].astype(jnp.float32) * resid[:, cols]).astype(jnp.bfloat16)
            for part in range(2):
                reach = weighted[part * low_b:part * low_b + WINDOW]
                back = jnp.dot(bw[k, part], reach, preferred_element_type=jnp.float32)
                cb[k, pl.ds(part * half, half), ahead] = back.astype(cb.dtype)

        @pl.loop(step * per, step * per + per)
        def _(rank):
            window_sum(rank)

            @pl.when(rank > 0)
            def _():
                send_term(rank - 1)

    window_sum(count)
    send_term(count - 1)

    for c in range(grad_ref.shape[0]):
        grad_ref[c] = jnp.where(owned(me, c), leaving[me].astype(jnp.float32), 0.0)
    for rank in range(count):
        e = reversed_order(rank, count)

        @pl.when(e != me)
        def _():
            pltpu.make_async_copy(leaving.at[0], arrived.at[e], term_recv.at[e]).wait()
            value = arrived[e].astype(jnp.float32)
            for c in range(grad_ref.shape[0]):
                grad_ref[c] += jnp.where(owned(e, c), value, 0.0)

    for e in range(count):
        @pl.when(e != me)
        def _():
            lat_copy(e).wait_send()
            term_copy(e).wait_send()
    for side, there in sends:
        @pl.when(there)
        def _():
            for copy in seen_copies(side):
                copy.wait_send()
            for c in range(chunks):
                halo_copies(c, side).wait_send()
            for b in range(count):
                rim_copy(b, side).wait_send()


def fused_body(latent, row_taps, column_taps, coefficients, observed, cell_of, valid_rows):
    kernels, tap_count = row_taps.shape
    half_width = tap_count // 2
    strip, width = observed.shape[1:]
    ncells = latent.shape[0]
    inner = round_up(half_width, PACK)
    outer = round_up(2 * half_width, PACK)
    count, row_count = lax.axis_size("exp"), lax.axis_size("row")

    vmem = pl.BlockSpec(memory_space=pltpu.VMEM)
    hbm = pl.BlockSpec(memory_space=pl.ANY)
    chunks = width // WINDOW
    block = strip // 2 + inner
    bf16 = jnp.bfloat16
    dma = pltpu.SemaphoreType.DMA
    dims = (count, row_count, kernels, tap_count, strip, width, inner, outer)
    residual, gradient = pl.pallas_call(
        functools.partial(fused_kernel, dims),
        out_shape=(
            jax.ShapeDtypeStruct((strip, width), jnp.float32),
            jax.ShapeDtypeStruct((ncells, strip, LANES), jnp.float32),
        ),
        in_specs=[vmem, vmem, vmem, vmem, vmem, hbm, hbm],
        out_specs=(vmem, vmem),
        scratch_shapes=[
            pltpu.VMEM((count, 8, LANES), jnp.int32),
            pltpu.VMEM((4, kernels, WINDOW), jnp.float32),
            pltpu.VMEM((kernels, strip + 2 * inner, width), bf16),
            pltpu.VMEM((strip + 2 * inner, width), bf16),
            pltpu.VMEM((strip + 2 * inner, LANES), bf16),
            pltpu.VMEM((count, strip, LANES), bf16),
            pltpu.VMEM((strip + 2 * outer, width + 2 * LANES), bf16),
            pltpu.VMEM((strip + 2 * outer, WINDOW + LANES), bf16),
            pltpu.VMEM((kernels // 2, WINDOW, 2 * LANES), bf16),
            pltpu.VMEM((kernels, WINDOW, LANES), bf16),
            pltpu.VMEM((kernels, 2, block, WINDOW), bf16),
            pltpu.VMEM((kernels, 2, strip // 2, WINDOW), bf16),
            pltpu.VMEM((kernels, strip + 2 * outer, WINDOW), bf16),
            pltpu.VMEM((strip + 2 * inner, width), jnp.float32),
            pltpu.VMEM((kernels, strip, width + 2 * LANES), bf16),
            pltpu.VMEM((strip, width + LANES), jnp.float32),
            pltpu.VMEM((count, strip, LANES), bf16),
            pltpu.VMEM((count, strip, LANES), bf16),
            dma((chunks + 2,)),
            dma((count,)), dma((count,)),
            dma((2, count)), dma((2, count)),
            dma((2, chunks + 2)), dma((2, chunks + 2)),
            dma((count,)), dma((count,)),
        ],
        compiler_params=pltpu.CompilerParams(
            vmem_limit_bytes=44 * 2**20, collective_id=0, has_side_effects=True),
        cost_estimate=pl.CostEstimate(flops=10**10, bytes_accessed=2 * 10**7, transcendentals=0),
    )(cell_of.reshape(1, count), latent, row_taps, column_taps, valid_rows, observed[0], coefficients[0])
    return (gradient, residual[None])


def body(latent, *others):
    if latent.shape[2] == LANES:
        return fused_body(latent, *others)
    return apart_body(latent, *others)


def solution(mesh):
    placed = (
        P(None, "row", "exp"),
        P(),
        P(),
        P("exp", None, "row", None),
        P("exp", "row", None),
        P(),
        P("exp", "row"),
    )
    return jax.shard_map(
        body,
        mesh=mesh,
        in_specs=placed,
        out_specs=(P(None, "row", "exp"), P("exp", "row", None)),
        check_vma=False,
    )
```

```python
import functools

import jax
import jax.numpy as jnp
from jax import lax
from jax.experimental import pallas as pl
from jax.experimental.pallas import tpu as pltpu
from jax.sharding import PartitionSpec as P

LANES = 128
WINDOW = 256
PACK = 16
STEP = 64
MESH = pl.DeviceIdType.MESH


def round_up(value, step):
    return -(-value // step) * step


def from_behind(block, axis, distance):
    devices = range(lax.axis_size(axis))
    route = [(i - distance, i) for i in devices if i - distance in devices]
    return lax.ppermute(block, axis, route)


def toeplitz(taps_row, rows, first):
    parts = []
    for at in range(0, rows, STEP):
        moved = pltpu.roll(jnp.broadcast_to(taps_row, (8, WINDOW)), (first + at) % WINDOW, 1)
        spread = jnp.broadcast_to(moved[:1], (min(STEP, rows - at), WINDOW))
        parts.append(pltpu.roll(spread, 0, 1, stride=1, stride_axis=0))
    return jnp.concatenate(parts, axis=0)


def filters_kernel(
    dims,
    lat_ref, taps_ref, obs_ref, mask_ref, coef_hbm, above_hbm, below_hbm,
    res_ref, term_ref,
    coef, lsh, fw, gw, aw, bw, rb, resid, cb, tsh, sems,
):
    kernels, tap_count, strip, width, inner, outer = dims
    half_width = tap_count // 2
    half = strip // 2
    block = half + inner
    chunks = width // WINDOW

    def copies(c):
        cols = pl.ds(c * WINDOW, WINDOW)
        return (
            pltpu.make_async_copy(
                coef_hbm.at[:, :, cols], coef.at[:, pl.ds(inner, strip), cols], sems.at[c, 0]),
            pltpu.make_async_copy(
                above_hbm.at[:, :, cols], coef.at[:, pl.ds(0, inner), cols], sems.at[c, 1]),
            pltpu.make_async_copy(
                below_hbm.at[:, :, cols], coef.at[:, pl.ds(inner + strip, inner), cols], sems.at[c, 2]),
        )

    for c in range(chunks):
        for copy in copies(c):
            copy.start()

    lsh[:, pl.ds(0, LANES)] = jnp.zeros((lsh.shape[0], LANES), lsh.dtype)
    lsh[:, pl.ds(width, LANES)] = jnp.zeros((lsh.shape[0], LANES), lsh.dtype)
    lsh[:, pl.ds(LANES // 2, width)] = lat_ref[...]

    low_a = strip + 2 * outer - WINDOW
    low_b = strip + 2 * inner - WINDOW
    side = LANES // 2 + half_width

    @pl.loop(0, kernels // 2)
    def _(pair):
        for odd in range(2):
            k = 2 * pair + odd
            row = taps_ref[0, pl.ds(k, 1), :]
            row_rev = taps_ref[1, pl.ds(k, 1), :]
            col = taps_ref[2, pl.ds(k, 1), :]
            col_rev = taps_ref[3, pl.ds(k, 1), :]
            shape = (pl.ds(odd * LANES, LANES))
            fw[pair, :, shape] = toeplitz(row_rev, WINDOW, -side)[:, :LANES].astype(fw.dtype)
            gw[k] = toeplitz(row, WINDOW, -side)[:, :LANES].astype(gw.dtype)
            aw[k, 0] = toeplitz(col, block, outer - inner - half_width).astype(aw.dtype)
            aw[k, 1] = toeplitz(col, block, half + outer - half_width - low_a).astype(aw.dtype)
            bw[k, 0] = toeplitz(col_rev, half, inner - half_width).astype(bw.dtype)
            bw[k, 1] = toeplitz(col_rev, half, half + inner - half_width - low_b).astype(bw.dtype)

    @pl.loop(0, chunks)
    def _(c):
        for copy in copies(c):
            copy.wait()
        start = pl.multiple_of(c * WINDOW, WINDOW)
        cols = pl.ds(start, WINDOW)
        for b in range(WINDOW // LANES):
            window = lsh[:, pl.ds(pl.multiple_of(start + b * LANES, LANES), WINDOW)]
            for pair in range(kernels // 2):
                both = jnp.dot(window, fw[pair], preferred_element_type=jnp.float32).astype(rb.dtype)
                rb[2 * pair, :, pl.ds(b * LANES, LANES)] = both[:, :LANES]
                rb[2 * pair + 1, :, pl.ds(b * LANES, LANES)] = both[:, LANES:]
        for part in range(2):
            rows = pl.ds(part * block, block)
            seen = pl.ds(part * low_a, WINDOW)
            predicted = jnp.zeros((block, WINDOW), jnp.float32)
            for k in range(kernels):
                vertical = jnp.dot(aw[k, part], rb[k, seen, :], preferred_element_type=jnp.float32)
                predicted += coef[k, rows, cols].astype(jnp.float32) * vertical
            mask = mask_ref[rows, :]
            mask = jnp.concatenate([mask] * (WINDOW // LANES), axis=1)
            resid[rows, :] = mask * (predicted - obs_ref[rows, cols].astype(jnp.float32))
        res_ref[:, cols] = resid[pl.ds(inner, strip), :]
        for k in range(kernels):
            weighted = (coef[k, :, cols].astype(jnp.float32) * resid[...]).astype(jnp.bfloat16)
            for part in range(2):
                seen = weighted[part * low_b:part * low_b + WINDOW]
                back = jnp.dot(bw[k, part], seen, preferred_element_type=jnp.float32)
                cb[k, pl.ds(part * half, half), cols] = back.astype(cb.dtype)

    blocks = width // LANES
    for out, source, taps_at in (
        (0, 0, LANES), (width, width - LANES, 0),
    ):
        total = jnp.zeros((strip, LANES), jnp.float32)
        for k in range(kernels):
            total += jnp.dot(
                cb[k, :, pl.ds(source, LANES)], gw[k, pl.ds(taps_at, LANES), :],
                preferred_element_type=jnp.float32)
        tsh[:, pl.ds(out, LANES)] = total

    @pl.loop(0, blocks - 1)
    def _(b):
        source = pl.multiple_of(b * LANES, LANES)
        total = jnp.zeros((strip, LANES), jnp.float32)
        for k in range(kernels):
            total += jnp.dot(
                cb[k, :, pl.ds(source, WINDOW)], gw[k], preferred_element_type=jnp.float32)
        tsh[:, pl.ds(pl.multiple_of(source + LANES, LANES), LANES)] = total

    term_ref[...] = tsh[:, pl.ds(LANES // 2, width)].astype(term_ref.dtype)


def apart_body(latent, row_taps, column_taps, coefficients, observed, cell_of, valid_rows):
    kernels, tap_count = row_taps.shape
    half_width = tap_count // 2
    strip, width = observed.shape[1:]
    ncells = latent.shape[0]
    inner = round_up(half_width, PACK)
    outer = round_up(2 * half_width, PACK)
    cell_list = cell_of[:, 0]

    above_coef = from_behind(coefficients[0, :, strip - inner:], "row", 1)
    below_coef = from_behind(coefficients[0, :, :inner], "row", -1)
    usable = jnp.broadcast_to(valid_rows[0].astype(jnp.bfloat16)[:, None], (strip, LANES))
    seen = jnp.concatenate([observed[0], usable], axis=1)
    seen = jnp.concatenate(
        [from_behind(seen[strip - inner:], "row", 1), seen, from_behind(seen[:inner], "row", -1)], axis=0)
    mask = seen[:, width:].astype(jnp.float32)
    seen = seen[:, :width]

    outgoing = jnp.take(latent, cell_list, axis=0)
    arrived = lax.all_to_all(outgoing, "exp", split_axis=0, concat_axis=2, tiled=True)[0]
    extended = jnp.concatenate(
        [from_behind(arrived[strip - outer:], "row", 1), arrived, from_behind(arrived[:outer], "row", -1)], axis=0)

    taps = jnp.stack([row_taps, row_taps[:, ::-1], column_taps, column_taps[:, ::-1]]).astype(jnp.float32)
    taps = jnp.pad(taps, ((0, 0), (0, 0), (0, WINDOW - tap_count)))

    vmem = pl.BlockSpec(memory_space=pltpu.VMEM)
    hbm = pl.BlockSpec(memory_space=pl.ANY)
    dims = (kernels, tap_count, strip, width, inner, outer)
    block = strip // 2 + inner
    bf16 = jnp.bfloat16
    residual, term = pl.pallas_call(
        functools.partial(filters_kernel, dims),
        out_shape=(
            jax.ShapeDtypeStruct((strip, width), jnp.float32),
            jax.ShapeDtypeStruct((strip, width), bf16),
        ),
        in_specs=[vmem, vmem, vmem, vmem, hbm, hbm, hbm],
        out_specs=(vmem, vmem),
        scratch_shapes=[
            pltpu.VMEM((kernels, strip + 2 * inner, width), bf16),
            pltpu.VMEM((strip + 2 * outer, width + LANES), bf16),
            pltpu.VMEM((kernels // 2, WINDOW, 2 * LANES), bf16),
            pltpu.VMEM((kernels, WINDOW, LANES), bf16),
            pltpu.VMEM((kernels, 2, block, WINDOW), bf16),
            pltpu.VMEM((kernels, 2, strip // 2, WINDOW), bf16),
            pltpu.VMEM((kernels, strip + 2 * outer, WINDOW), bf16),
            pltpu.VMEM((strip + 2 * inner, WINDOW), jnp.float32),
            pltpu.VMEM((kernels, strip, width), bf16),
            pltpu.VMEM((strip, width + LANES), jnp.float32),
            pltpu.SemaphoreType.DMA((width // WINDOW, 3)),
        ],
        compiler_params=pltpu.CompilerParams(vmem_limit_bytes=56 * 2**20),
        cost_estimate=pl.CostEstimate(flops=10**10, bytes_accessed=2 * 10**7, transcendentals=0),
    )(extended, taps, seen, mask, coefficients[0], above_coef, below_coef)

    incoming = lax.all_to_all(term[None], "exp", split_axis=2, concat_axis=0, tiled=True)
    owner = jnp.arange(ncells)[:, None] == cell_list[None, :]
    gradient = jnp.sum(
        jnp.where(owner[:, :, None, None], incoming[None].astype(jnp.float32), 0.0), axis=1)
    return (gradient, residual[None])


def fused_kernel(
    dims,
    cells_hbm, lat_hbm, along_hbm, down_hbm, valid_hbm, obs_hbm, coef_hbm,
    res_ref, grad_ref,
    cells_ref, lat_ref, along_ref, down_ref, valid_ref, cells, taps_ref, coef, seen, usable, outgoing, lat, lsh, fw, gw, ew, aw, bw, resid, tot, stray, leaving, arrived,
    own_sems, lat_send, lat_recv, rim_send, rim_recv, halo_send, halo_recv, term_send, term_recv,
):
    count, row_count, kernels, tap_count, strip, width, inner, outer = dims
    half_width = tap_count // 2
    half = strip // 2
    block = half + inner
    chunks = width // WINDOW
    per = WINDOW // LANES
    me = lax.axis_index("exp")
    row = lax.axis_index("row")
    rising = me < count // 2
    has_above = row > 0
    has_below = row < row_count - 1

    def ordered(rank, length):
        return jnp.where(rising, rank, length - 1 - rank)

    def reversed_order(rank, length):
        return jnp.where(rising, length - 1 - rank, rank)

    def lane_block(b):
        return pl.ds(pl.multiple_of(b * LANES, LANES), LANES)

    def chunk_cols(c):
        return pl.ds(pl.multiple_of(c * WINDOW, WINDOW), WINDOW)

    barrier = pltpu.get_barrier_semaphore()
    for e in range(count):
        @pl.when(e != me)
        def _():
            pl.semaphore_signal(barrier, inc=1, device_id={"exp": e}, device_id_type=MESH)

    @pl.when(has_above)
    def _():
        pl.semaphore_signal(barrier, inc=1, device_id={"row": row - 1}, device_id_type=MESH)

    @pl.when(has_below)
    def _():
        pl.semaphore_signal(barrier, inc=1, device_id={"row": row + 1}, device_id_type=MESH)

    def own_coef(c):
        cols = chunk_cols(c)
        return pltpu.make_async_copy(
            coef_hbm.at[:, :, cols], coef.at[:, pl.ds(inner, strip), cols], own_sems.at[c])

    own_seen = pltpu.make_async_copy(obs_hbm, seen.at[pl.ds(inner, strip)], own_sems.at[chunks])
    fetched = [
        pltpu.make_async_copy(src, dst, own_sems.at[chunks + 1 + i])
        for i, (src, dst) in enumerate((
            (cells_hbm, cells_ref), (lat_hbm, lat_ref), (along_hbm, along_ref),
            (down_hbm, down_ref), (valid_hbm, valid_ref)))]
    for copy in fetched:
        copy.start()
    own_seen.start()
    for step in range(chunks):
        own_coef(ordered(step, chunks)).start()

    for copy in fetched:
        copy.wait()
    for e in range(count):
        cells[e] = jnp.broadcast_to(cells_ref[:, e:e + 1], (8, LANES))

    def owned(e, c):
        return jnp.concatenate([(cells[e] == c).astype(jnp.float32)] * (strip // 8), axis=0) > 0.5

    for e in range(count):
        chosen = lat_ref[0].astype(jnp.float32)
        for c in range(1, lat_ref.shape[0]):
            chosen = jnp.where(owned(e, c), lat_ref[c].astype(jnp.float32), chosen)
        outgoing[e] = chosen.astype(outgoing.dtype)
    at_row = lax.broadcasted_iota(jnp.int32, (strip, strip), 0)
    at_col = lax.broadcasted_iota(jnp.int32, (strip, strip), 1)
    spread = jnp.where(at_row == at_col, valid_ref[...], 0).astype(jnp.bfloat16)
    usable[pl.ds(inner, strip), :] = jnp.dot(
        spread, jnp.ones((strip, LANES), jnp.bfloat16),
        preferred_element_type=jnp.float32).astype(usable.dtype)
    for ref in (lat,):
        ref[:, pl.ds(0, LANES)] = jnp.zeros((ref.shape[0], LANES), ref.dtype)
        ref[:, pl.ds(LANES + width, LANES)] = jnp.zeros((ref.shape[0], LANES), ref.dtype)

    def fill(at_lat, at_inner):
        lat[pl.ds(at_lat, outer), :] = jnp.zeros((outer, lat.shape[1]), lat.dtype)
        coef[:, pl.ds(at_inner, inner), :] = jnp.zeros((kernels, inner, width), coef.dtype)
        seen[pl.ds(at_inner, inner), :] = jnp.zeros((inner, width), seen.dtype)
        usable[pl.ds(at_inner, inner), :] = jnp.zeros((inner, LANES), usable.dtype)

    @pl.when(jnp.logical_not(has_above))
    def _():
        fill(0, 0)

    @pl.when(jnp.logical_not(has_below))
    def _():
        fill(outer + strip, inner + strip)

    pl.semaphore_wait(barrier, count - 1 + has_above.astype(jnp.int32) + has_below.astype(jnp.int32))

    strip_rows = pl.ds(outer, strip)

    def lat_copy(e):
        return pltpu.make_async_remote_copy(
            src_ref=outgoing.at[e], dst_ref=lat.at[strip_rows, lane_block(me + 1)],
            send_sem=lat_send.at[e], recv_sem=lat_recv.at[me],
            device_id={"exp": e}, device_id_type=MESH)

    def own_lat():
        return pltpu.make_async_copy(
            outgoing.at[me], lat.at[strip_rows, lane_block(me + 1)], lat_recv.at[me])

    def halo_copies(c, side):
        cols = chunk_cols(c)
        source = pl.ds(0 if side == 0 else strip - inner, inner)
        target = pl.ds(inner + strip if side == 0 else 0, inner)
        return pltpu.make_async_remote_copy(
            src_ref=coef_hbm.at[:, source, cols], dst_ref=coef.at[:, target, cols],
            send_sem=halo_send.at[side, c], recv_sem=halo_recv.at[side, c],
            device_id={"row": row - 1 if side == 0 else row + 1}, device_id_type=MESH)

    def seen_copies(side):
        source = 0 if side == 0 else strip - inner
        target = pl.ds(inner + strip if side == 0 else 0, inner)
        return [pltpu.make_async_remote_copy(
            src_ref=src.at[pl.ds(first + source, inner)], dst_ref=dst.at[target],
            send_sem=halo_send.at[side, chunks + i], recv_sem=halo_recv.at[side, chunks + i],
            device_id={"row": row - 1 if side == 0 else row + 1}, device_id_type=MESH)
            for i, (src, first, dst) in enumerate(((obs_hbm, 0, seen), (usable, inner, usable)))]

    def rim_copy(b, side):
        cols = lane_block(b + 1)
        source = pl.ds(outer if side == 0 else strip, outer)
        target = pl.ds(outer + strip if side == 0 else 0, outer)
        return pltpu.make_async_remote_copy(
            src_ref=lat.at[source, cols], dst_ref=lat.at[target, cols],
            send_sem=rim_send.at[side, b], recv_sem=rim_recv.at[side, b],
            device_id={"row": row - 1 if side == 0 else row + 1}, device_id_type=MESH)

    sends = ((0, has_above), (1, has_below))
    receives = ((0, has_below), (1, has_above))

    def start_halos(step):
        for side, there in sends:
            @pl.when(there)
            def _():
                halo_copies(ordered(step, chunks), side).start()

    late = ordered(me, count) < count // 4
    own_lat().start()
    for rank in range(count):
        e = ordered(rank, count)
        @pl.when(jnp.logical_and(e != me, jnp.logical_or(jnp.logical_not(late), rank < count // 2)))
        def _():
            lat_copy(e).start()
    start_halos(0)
    for side, there in sends:
        @pl.when(there)
        def _():
            for copy in seen_copies(side):
                copy.start()

    low_a = strip + 2 * outer - WINDOW
    low_b = strip + 2 * inner - WINDOW
    shift = LANES // 2 + half_width

    at_tap = lax.broadcasted_iota(jnp.int32, (tap_count, WINDOW), 0)
    at_lane = lax.broadcasted_iota(jnp.int32, (tap_count, WINDOW), 1)
    keep = (at_tap == at_lane).astype(jnp.float32).astype(jnp.bfloat16)
    turn = (at_tap + at_lane == tap_count - 1).astype(jnp.float32).astype(jnp.bfloat16)
    for i, (taps, order) in enumerate(((along_ref, keep), (along_ref, turn), (down_ref, keep), (down_ref, turn))):
        taps_ref[i] = jnp.dot(taps[...], order, preferred_element_type=jnp.float32)

    far = (
        lax.broadcasted_iota(jnp.int32, (WINDOW, WINDOW), 0)
        - lax.broadcasted_iota(jnp.int32, (WINDOW, WINDOW), 1))
    corner = jnp.abs(far) >= LANES

    @pl.loop(0, kernels // 2)
    def _(pair):
        for odd in range(2):
            k = 2 * pair + odd
            along = taps_ref[0, pl.ds(k, 1), :]
            along_rev = taps_ref[1, pl.ds(k, 1), :]
            down = taps_ref[2, pl.ds(k, 1), :]
            down_rev = taps_ref[3, pl.ds(k, 1), :]
            fw[pair, :, pl.ds(odd * LANES, LANES)] = toeplitz(along_rev, WINDOW, -shift)[:, :LANES].astype(fw.dtype)
            ring = toeplitz(along, WINDOW, -half_width)
            gw[k] = jnp.where(corner, 0.0, ring).astype(gw.dtype)
            reach = jnp.where(corner, ring, 0.0)
            reach = reach[:, :LANES] + reach[:, LANES:]
            ew[pair, pl.ds(odd * LANES, LANES // 2), :] = reach[:LANES // 2].astype(ew.dtype)
            ew[pair, pl.ds(odd * LANES + LANES // 2, LANES // 2), :] = reach[WINDOW - LANES // 2:].astype(ew.dtype)
            aw[k, 0] = toeplitz(down, block, outer - inner - half_width).astype(aw.dtype)
            aw[k, 1] = toeplitz(down, block, half + outer - half_width - low_a).astype(aw.dtype)
            bw[k, 0] = toeplitz(down_rev, half, inner - half_width).astype(bw.dtype)
            bw[k, 1] = toeplitz(down_rev, half, half + inner - half_width - low_b).astype(bw.dtype)

    for at in (0, chunks + 1):
        stray[at] = jnp.zeros((strip, LANES), stray.dtype)

    def take_block(rank):
        b = ordered(rank, count)
        pltpu.make_async_copy(
            outgoing.at[0], lat.at[strip_rows, lane_block(b + 1)], lat_recv.at[b]).wait()
        for side, there in sends:
            @pl.when(there)
            def _():
                rim_copy(b, side).start()

    def take_rims(rank):
        b = ordered(rank, count)
        for side, there in receives:
            @pl.when(there)
            def _():
                rim_copy(b, side).wait_recv()

    for rank in range(count // 2, count):
        @pl.when(late)
        def _():
            lat_copy(ordered(rank, count)).start()
    for rank in range(per + 1):
        take_block(rank)
    own_seen.wait()
    for side, there in receives:
        @pl.when(there)
        def _():
            for copy in seen_copies(side):
                copy.wait_recv()
    take_rims(0)

    @pl.loop(0, chunks)
    def _(step):
        c = ordered(step, chunks)
        cols = chunk_cols(c)

        @pl.when(step + 1 < chunks)
        def _():
            start_halos(step + 1)

        for more in range(1, per + 1):
            @pl.when(step * per + more < count)
            def _():
                take_rims(step * per + more)
        near = lat[:, pl.ds(pl.multiple_of(c * WINDOW, WINDOW), WINDOW + 2 * LANES)]
        lsh[...] = near[:, LANES // 2:LANES // 2 + WINDOW + LANES]
        own_coef(c).wait()
        for side, there in receives:
            @pl.when(there)
            def _():
                halo_copies(c, side).wait_recv()
        windows = [lsh[:, b * LANES:b * LANES + WINDOW] for b in range(per)]

        def predict(pairs, predicted):
            for pair in pairs:
                both = [
                    jnp.dot(window, fw[pair], preferred_element_type=jnp.float32).astype(jnp.bfloat16)
                    for window in windows]
                for odd in range(2):
                    k = 2 * pair + odd
                    blurred = jnp.concatenate(
                        [found[:, odd * LANES:(odd + 1) * LANES] for found in both], axis=1)
                    for part in range(2):
                        vertical = jnp.dot(
                            aw[k, part], blurred[part * low_a:part * low_a + WINDOW],
                            preferred_element_type=jnp.float32)
                        gain = coef[k, pl.ds(part * block, block), cols].astype(jnp.float32)
                        predicted[part] = predicted[part] + gain * vertical
            return predicted

        predicted = predict(range(kernels // 4), [jnp.zeros((block, WINDOW), jnp.float32)] * 2)
        for part in range(2):
            resid[pl.ds(part * block, block), cols] = predicted[part]
        for more in range(1, per + 1):
            @pl.when((step + 1) * per + more < count)
            def _():
                take_block((step + 1) * per + more)
        predicted = [resid[pl.ds(part * block, block), cols] for part in range(2)]
        predicted = predict(range(kernels // 4, kernels // 2), predicted)
        for part in range(2):
            rows = pl.ds(part * block, block)
            mask = usable[rows, :].astype(jnp.float32)
            mask = jnp.concatenate([mask] * per, axis=1)
            resid[rows, cols] = mask * (predicted[part] - seen[rows, cols].astype(jnp.float32))
        res_ref[:, cols] = resid[pl.ds(inner, strip), cols]

    def term_copy(b):
        return pltpu.make_async_remote_copy(
            src_ref=leaving.at[b], dst_ref=arrived.at[me],
            send_sem=term_send.at[b], recv_sem=term_recv.at[me],
            device_id={"exp": b}, device_id_type=MESH)

    lane_side = lax.broadcasted_iota(jnp.int32, (strip, LANES), 1) // (LANES // 2)

    def send_term(rank):
        b = reversed_order(rank, count)
        c, side = b // per, b % per
        beside = stray[jnp.where(side == 0, c, c + 2)]
        term = tot[:, lane_block(b)] + jnp.where(lane_side == side, beside, 0.0)
        leaving[b] = term.astype(leaving.dtype)

        @pl.when(b != me)
        def _():
            term_copy(b).start()

    @pl.loop(0, chunks)
    def _(step):
        c = reversed_order(step, chunks)
        cols = chunk_cols(c)
        inside = jnp.zeros((strip, WINDOW), jnp.float32)
        outside = jnp.zeros((strip, LANES), jnp.float32)
        left = lax.broadcasted_iota(jnp.int32, (strip, LANES), 1) < LANES // 2
        for pair in range(kernels // 2):
            edges = []
            for odd in range(2):
                k = 2 * pair + odd
                weighted = (coef[k, :, cols].astype(jnp.float32) * resid[:, cols]).astype(jnp.bfloat16)
                back = jnp.concatenate([
                    jnp.dot(
                        bw[k, part], weighted[part * low_b:part * low_b + WINDOW],
                        preferred_element_type=jnp.float32).astype(jnp.bfloat16)
                    for part in range(2)], axis=0)
                inside += jnp.dot(back, gw[k], preferred_element_type=jnp.float32)
                edges.append(jnp.where(left, back[:, :LANES], back[:, LANES:]))
            outside += jnp.dot(
                jnp.concatenate(edges, axis=1), ew[pair], preferred_element_type=jnp.float32)
        tot[:, cols] = inside
        stray[c + 1] = outside

        @pl.when(step > 0)
        def _():
            send_term(step * per - 1)

        send_term(step * per)

    send_term(count - 1)

    for c in range(grad_ref.shape[0]):
        grad_ref[c] = jnp.where(owned(me, c), leaving[me].astype(jnp.float32), 0.0)
    for rank in range(count):
        e = reversed_order(rank, count)

        @pl.when(e != me)
        def _():
            pltpu.make_async_copy(leaving.at[0], arrived.at[e], term_recv.at[e]).wait()
            value = arrived[e].astype(jnp.float32)
            for c in range(grad_ref.shape[0]):
                grad_ref[c] += jnp.where(owned(e, c), value, 0.0)

    for e in range(count):
        @pl.when(e != me)
        def _():
            lat_copy(e).wait_send()
            term_copy(e).wait_send()
    for side, there in sends:
        @pl.when(there)
        def _():
            for copy in seen_copies(side):
                copy.wait_send()
            for c in range(chunks):
                halo_copies(c, side).wait_send()
            for b in range(count):
                rim_copy(b, side).wait_send()


def fused_body(latent, row_taps, column_taps, coefficients, observed, cell_of, valid_rows):
    kernels, tap_count = row_taps.shape
    half_width = tap_count // 2
    strip, width = observed.shape[1:]
    ncells = latent.shape[0]
    inner = round_up(half_width, PACK)
    outer = round_up(2 * half_width, PACK)
    count, row_count = lax.axis_size("exp"), lax.axis_size("row")

    vmem = pl.BlockSpec(memory_space=pltpu.VMEM)
    hbm = pl.BlockSpec(memory_space=pltpu.HBM)
    chunks = width // WINDOW
    block = strip // 2 + inner
    bf16 = jnp.bfloat16
    dma = pltpu.SemaphoreType.DMA
    dims = (count, row_count, kernels, tap_count, strip, width, inner, outer)
    residual, gradient = pl.pallas_call(
        functools.partial(fused_kernel, dims),
        out_shape=(
            jax.ShapeDtypeStruct((strip, width), jnp.float32),
            jax.ShapeDtypeStruct((ncells, strip, LANES), jnp.float32),
        ),
        in_specs=[hbm] * 7,
        out_specs=(vmem, vmem),
        scratch_shapes=[
            pltpu.VMEM((1, count), jnp.int32),
            pltpu.VMEM((ncells, strip, LANES), bf16),
            pltpu.VMEM((kernels, tap_count), bf16),
            pltpu.VMEM((kernels, tap_count), bf16),
            pltpu.VMEM((1, strip), jnp.int32),
            pltpu.VMEM((count, 8, LANES), jnp.int32),
            pltpu.VMEM((4, kernels, WINDOW), jnp.float32),
            pltpu.VMEM((kernels, strip + 2 * inner, width), bf16),
            pltpu.VMEM((strip + 2 * inner, width), bf16),
            pltpu.VMEM((strip + 2 * inner, LANES), bf16),
            pltpu.VMEM((count, strip, LANES), bf16),
            pltpu.VMEM((strip + 2 * outer, width + 2 * LANES), bf16),
            pltpu.VMEM((strip + 2 * outer, WINDOW + LANES), bf16),
            pltpu.VMEM((kernels // 2, WINDOW, 2 * LANES), bf16),
            pltpu.VMEM((kernels, WINDOW, WINDOW), bf16),
            pltpu.VMEM((kernels // 2, WINDOW, LANES), bf16),
            pltpu.VMEM((kernels, 2, block, WINDOW), bf16),
            pltpu.VMEM((kernels, 2, strip // 2, WINDOW), bf16),
            pltpu.VMEM((strip + 2 * inner, width), jnp.float32),
            pltpu.VMEM((strip, width), jnp.float32),
            pltpu.VMEM((chunks + 2, strip, LANES), jnp.float32),
            pltpu.VMEM((count, strip, LANES), bf16),
            pltpu.VMEM((count, strip, LANES), bf16),
            dma((chunks + 6,)),
            dma((count,)), dma((count,)),
            dma((2, count)), dma((2, count)),
            dma((2, chunks + 2)), dma((2, chunks + 2)),
            dma((count,)), dma((count,)),
        ],
        compiler_params=pltpu.CompilerParams(
            vmem_limit_bytes=44 * 2**20, collective_id=0, has_side_effects=True),
        cost_estimate=pl.CostEstimate(flops=10**10, bytes_accessed=2 * 10**7, transcendentals=0),
    )(*[pltpu.with_memory_space_constraint(x, pltpu.HBM) for x in (
        cell_of.reshape(1, count), latent, row_taps, column_taps, valid_rows, observed[0], coefficients[0])])
    return (gradient, residual[None])


def body(latent, *others):
    if latent.shape[2] == LANES:
        return fused_body(latent, *others)
    return apart_body(latent, *others)


def solution(mesh):
    placed = (
        P(None, "row", "exp"),
        P(),
        P(),
        P("exp", None, "row", None),
        P("exp", "row", None),
        P(),
        P("exp", "row"),
    )
    return jax.shard_map(
        body,
        mesh=mesh,
        in_specs=placed,
        out_specs=(P(None, "row", "exp"), P("exp", "row", None)),
        check_vma=False,
    )
```

```python
import functools

import jax
import jax.numpy as jnp
from jax import lax
from jax.experimental import pallas as pl
from jax.experimental.pallas import tpu as pltpu
from jax.sharding import PartitionSpec as P

LANES = 128
WINDOW = 256
PACK = 16
STEP = 64
MESH = pl.DeviceIdType.MESH


def round_up(value, step):
    return -(-value // step) * step


def from_behind(block, axis, distance):
    devices = range(lax.axis_size(axis))
    route = [(i - distance, i) for i in devices if i - distance in devices]
    return lax.ppermute(block, axis, route)


def toeplitz(taps_row, rows, first):
    parts = []
    for at in range(0, rows, STEP):
        moved = pltpu.roll(jnp.broadcast_to(taps_row, (8, WINDOW)), (first + at) % WINDOW, 1)
        spread = jnp.broadcast_to(moved[:1], (min(STEP, rows - at), WINDOW))
        parts.append(pltpu.roll(spread, 0, 1, stride=1, stride_axis=0))
    return jnp.concatenate(parts, axis=0)


def filters_kernel(
    dims,
    lat_ref, taps_ref, obs_ref, mask_ref, coef_hbm, above_hbm, below_hbm,
    res_ref, term_ref,
    coef, lsh, fw, gw, aw, bw, rb, resid, cb, tsh, sems,
):
    kernels, tap_count, strip, width, inner, outer = dims
    half_width = tap_count // 2
    half = strip // 2
    block = half + inner
    chunks = width // WINDOW

    def copies(c):
        cols = pl.ds(c * WINDOW, WINDOW)
        return (
            pltpu.make_async_copy(
                coef_hbm.at[:, :, cols], coef.at[:, pl.ds(inner, strip), cols], sems.at[c, 0]),
            pltpu.make_async_copy(
                above_hbm.at[:, :, cols], coef.at[:, pl.ds(0, inner), cols], sems.at[c, 1]),
            pltpu.make_async_copy(
                below_hbm.at[:, :, cols], coef.at[:, pl.ds(inner + strip, inner), cols], sems.at[c, 2]),
        )

    for c in range(chunks):
        for copy in copies(c):
            copy.start()

    lsh[:, pl.ds(0, LANES)] = jnp.zeros((lsh.shape[0], LANES), lsh.dtype)
    lsh[:, pl.ds(width, LANES)] = jnp.zeros((lsh.shape[0], LANES), lsh.dtype)
    lsh[:, pl.ds(LANES // 2, width)] = lat_ref[...]

    low_a = strip + 2 * outer - WINDOW
    low_b = strip + 2 * inner - WINDOW
    side = LANES // 2 + half_width

    @pl.loop(0, kernels // 2)
    def _(pair):
        for odd in range(2):
            k = 2 * pair + odd
            row = taps_ref[0, pl.ds(k, 1), :]
            row_rev = taps_ref[1, pl.ds(k, 1), :]
            col = taps_ref[2, pl.ds(k, 1), :]
            col_rev = taps_ref[3, pl.ds(k, 1), :]
            shape = (pl.ds(odd * LANES, LANES))
            fw[pair, :, shape] = toeplitz(row_rev, WINDOW, -side)[:, :LANES].astype(fw.dtype)
            gw[k] = toeplitz(row, WINDOW, -side)[:, :LANES].astype(gw.dtype)
            aw[k, 0] = toeplitz(col, block, outer - inner - half_width).astype(aw.dtype)
            aw[k, 1] = toeplitz(col, block, half + outer - half_width - low_a).astype(aw.dtype)
            bw[k, 0] = toeplitz(col_rev, half, inner - half_width).astype(bw.dtype)
            bw[k, 1] = toeplitz(col_rev, half, half + inner - half_width - low_b).astype(bw.dtype)

    @pl.loop(0, chunks)
    def _(c):
        for copy in copies(c):
            copy.wait()
        start = pl.multiple_of(c * WINDOW, WINDOW)
        cols = pl.ds(start, WINDOW)
        for b in range(WINDOW // LANES):
            window = lsh[:, pl.ds(pl.multiple_of(start + b * LANES, LANES), WINDOW)]
            for pair in range(kernels // 2):
                both = jnp.dot(window, fw[pair], preferred_element_type=jnp.float32).astype(rb.dtype)
                rb[2 * pair, :, pl.ds(b * LANES, LANES)] = both[:, :LANES]
                rb[2 * pair + 1, :, pl.ds(b * LANES, LANES)] = both[:, LANES:]
        for part in range(2):
            rows = pl.ds(part * block, block)
            seen = pl.ds(part * low_a, WINDOW)
            predicted = jnp.zeros((block, WINDOW), jnp.float32)
            for k in range(kernels):
                vertical = jnp.dot(aw[k, part], rb[k, seen, :], preferred_element_type=jnp.float32)
                predicted += coef[k, rows, cols].astype(jnp.float32) * vertical
            mask = mask_ref[rows, :]
            mask = jnp.concatenate([mask] * (WINDOW // LANES), axis=1)
            resid[rows, :] = mask * (predicted - obs_ref[rows, cols].astype(jnp.float32))
        res_ref[:, cols] = resid[pl.ds(inner, strip), :]
        for k in range(kernels):
            weighted = (coef[k, :, cols].astype(jnp.float32) * resid[...]).astype(jnp.bfloat16)
            for part in range(2):
                seen = weighted[part * low_b:part * low_b + WINDOW]
                back = jnp.dot(bw[k, part], seen, preferred_element_type=jnp.float32)
                cb[k, pl.ds(part * half, half), cols] = back.astype(cb.dtype)

    blocks = width // LANES
    for out, source, taps_at in (
        (0, 0, LANES), (width, width - LANES, 0),
    ):
        total = jnp.zeros((strip, LANES), jnp.float32)
        for k in range(kernels):
            total += jnp.dot(
                cb[k, :, pl.ds(source, LANES)], gw[k, pl.ds(taps_at, LANES), :],
                preferred_element_type=jnp.float32)
        tsh[:, pl.ds(out, LANES)] = total

    @pl.loop(0, blocks - 1)
    def _(b):
        source = pl.multiple_of(b * LANES, LANES)
        total = jnp.zeros((strip, LANES), jnp.float32)
        for k in range(kernels):
            total += jnp.dot(
                cb[k, :, pl.ds(source, WINDOW)], gw[k], preferred_element_type=jnp.float32)
        tsh[:, pl.ds(pl.multiple_of(source + LANES, LANES), LANES)] = total

    term_ref[...] = tsh[:, pl.ds(LANES // 2, width)].astype(term_ref.dtype)


def apart_body(latent, row_taps, column_taps, coefficients, observed, cell_of, valid_rows):
    kernels, tap_count = row_taps.shape
    half_width = tap_count // 2
    strip, width = observed.shape[1:]
    ncells = latent.shape[0]
    inner = round_up(half_width, PACK)
    outer = round_up(2 * half_width, PACK)
    cell_list = cell_of[:, 0]

    above_coef = from_behind(coefficients[0, :, strip - inner:], "row", 1)
    below_coef = from_behind(coefficients[0, :, :inner], "row", -1)
    usable = jnp.broadcast_to(valid_rows[0].astype(jnp.bfloat16)[:, None], (strip, LANES))
    seen = jnp.concatenate([observed[0], usable], axis=1)
    seen = jnp.concatenate(
        [from_behind(seen[strip - inner:], "row", 1), seen, from_behind(seen[:inner], "row", -1)], axis=0)
    mask = seen[:, width:].astype(jnp.float32)
    seen = seen[:, :width]

    outgoing = jnp.take(latent, cell_list, axis=0)
    arrived = lax.all_to_all(outgoing, "exp", split_axis=0, concat_axis=2, tiled=True)[0]
    extended = jnp.concatenate(
        [from_behind(arrived[strip - outer:], "row", 1), arrived, from_behind(arrived[:outer], "row", -1)], axis=0)

    taps = jnp.stack([row_taps, row_taps[:, ::-1], column_taps, column_taps[:, ::-1]]).astype(jnp.float32)
    taps = jnp.pad(taps, ((0, 0), (0, 0), (0, WINDOW - tap_count)))

    vmem = pl.BlockSpec(memory_space=pltpu.VMEM)
    hbm = pl.BlockSpec(memory_space=pl.ANY)
    dims = (kernels, tap_count, strip, width, inner, outer)
    block = strip // 2 + inner
    bf16 = jnp.bfloat16
    residual, term = pl.pallas_call(
        functools.partial(filters_kernel, dims),
        out_shape=(
            jax.ShapeDtypeStruct((strip, width), jnp.float32),
            jax.ShapeDtypeStruct((strip, width), bf16),
        ),
        in_specs=[vmem, vmem, vmem, vmem, hbm, hbm, hbm],
        out_specs=(vmem, vmem),
        scratch_shapes=[
            pltpu.VMEM((kernels, strip + 2 * inner, width), bf16),
            pltpu.VMEM((strip + 2 * outer, width + LANES), bf16),
            pltpu.VMEM((kernels // 2, WINDOW, 2 * LANES), bf16),
            pltpu.VMEM((kernels, WINDOW, LANES), bf16),
            pltpu.VMEM((kernels, 2, block, WINDOW), bf16),
            pltpu.VMEM((kernels, 2, strip // 2, WINDOW), bf16),
            pltpu.VMEM((kernels, strip + 2 * outer, WINDOW), bf16),
            pltpu.VMEM((strip + 2 * inner, WINDOW), jnp.float32),
            pltpu.VMEM((kernels, strip, width), bf16),
            pltpu.VMEM((strip, width + LANES), jnp.float32),
            pltpu.SemaphoreType.DMA((width // WINDOW, 3)),
        ],
        compiler_params=pltpu.CompilerParams(vmem_limit_bytes=56 * 2**20),
        cost_estimate=pl.CostEstimate(flops=10**10, bytes_accessed=2 * 10**7, transcendentals=0),
    )(extended, taps, seen, mask, coefficients[0], above_coef, below_coef)

    incoming = lax.all_to_all(term[None], "exp", split_axis=2, concat_axis=0, tiled=True)
    owner = jnp.arange(ncells)[:, None] == cell_list[None, :]
    gradient = jnp.sum(
        jnp.where(owner[:, :, None, None], incoming[None].astype(jnp.float32), 0.0), axis=1)
    return (gradient, residual[None])


def fused_kernel(
    dims,
    cells_hbm, lat_hbm, along_hbm, down_hbm, valid_hbm, obs_hbm, coef_hbm,
    res_ref, grad_ref,
    cells_ref, lat_ref, along_ref, down_ref, valid_ref, cells, taps_ref, coef, seen, usable, outgoing, lat, lsh, fw, gw, ew, aw, bw, rb, resid, tot, stray, leaving, arrived,
    own_sems, lat_send, lat_recv, rim_send, rim_recv, halo_send, halo_recv, term_send, term_recv,
):
    count, row_count, kernels, tap_count, strip, width, inner, outer = dims
    half_width = tap_count // 2
    half = strip // 2
    block = half + inner
    chunks = width // WINDOW
    per = WINDOW // LANES
    me = lax.axis_index("exp")
    row = lax.axis_index("row")
    rising = me < count // 2
    has_above = row > 0
    has_below = row < row_count - 1

    def ordered(rank, length):
        return jnp.where(rising, rank, length - 1 - rank)

    def reversed_order(rank, length):
        return jnp.where(rising, length - 1 - rank, rank)

    def lane_block(b):
        return pl.ds(pl.multiple_of(b * LANES, LANES), LANES)

    def chunk_cols(c):
        return pl.ds(pl.multiple_of(c * WINDOW, WINDOW), WINDOW)

    barrier = pltpu.get_barrier_semaphore()
    for e in range(count):
        @pl.when(e != me)
        def _():
            pl.semaphore_signal(barrier, inc=1, device_id={"exp": e}, device_id_type=MESH)

    @pl.when(has_above)
    def _():
        pl.semaphore_signal(barrier, inc=1, device_id={"row": row - 1}, device_id_type=MESH)

    @pl.when(has_below)
    def _():
        pl.semaphore_signal(barrier, inc=1, device_id={"row": row + 1}, device_id_type=MESH)

    def own_coef(c):
        cols = chunk_cols(c)
        return pltpu.make_async_copy(
            coef_hbm.at[:, :, cols], coef.at[:, pl.ds(inner, strip), cols], own_sems.at[c])

    own_seen = pltpu.make_async_copy(obs_hbm, seen.at[pl.ds(inner, strip)], own_sems.at[chunks])
    fetched = [
        pltpu.make_async_copy(src, dst, own_sems.at[chunks + 1 + i])
        for i, (src, dst) in enumerate((
            (cells_hbm, cells_ref), (lat_hbm, lat_ref), (along_hbm, along_ref),
            (down_hbm, down_ref), (valid_hbm, valid_ref)))]
    for copy in fetched:
        copy.start()
    own_seen.start()
    for step in range(chunks):
        own_coef(ordered(step, chunks)).start()

    for copy in fetched:
        copy.wait()
    for e in range(count):
        cells[e] = jnp.broadcast_to(cells_ref[:, e:e + 1], (8, LANES))

    def owned(e, c):
        return jnp.concatenate([(cells[e] == c).astype(jnp.float32)] * (strip // 8), axis=0) > 0.5

    for e in range(count):
        chosen = lat_ref[0].astype(jnp.float32)
        for c in range(1, lat_ref.shape[0]):
            chosen = jnp.where(owned(e, c), lat_ref[c].astype(jnp.float32), chosen)
        outgoing[e] = chosen.astype(outgoing.dtype)
    at_row = lax.broadcasted_iota(jnp.int32, (strip, strip), 0)
    at_col = lax.broadcasted_iota(jnp.int32, (strip, strip), 1)
    spread = jnp.where(at_row == at_col, valid_ref[...], 0).astype(jnp.bfloat16)
    usable[pl.ds(inner, strip), :] = jnp.dot(
        spread, jnp.ones((strip, LANES), jnp.bfloat16),
        preferred_element_type=jnp.float32).astype(usable.dtype)
    for ref in (lat,):
        ref[:, pl.ds(0, LANES)] = jnp.zeros((ref.shape[0], LANES), ref.dtype)
        ref[:, pl.ds(LANES + width, LANES)] = jnp.zeros((ref.shape[0], LANES), ref.dtype)

    def fill(at_lat, at_inner):
        lat[pl.ds(at_lat, outer), :] = jnp.zeros((outer, lat.shape[1]), lat.dtype)
        coef[:, pl.ds(at_inner, inner), :] = jnp.zeros((kernels, inner, width), coef.dtype)
        seen[pl.ds(at_inner, inner), :] = jnp.zeros((inner, width), seen.dtype)
        usable[pl.ds(at_inner, inner), :] = jnp.zeros((inner, LANES), usable.dtype)

    @pl.when(jnp.logical_not(has_above))
    def _():
        fill(0, 0)

    @pl.when(jnp.logical_not(has_below))
    def _():
        fill(outer + strip, inner + strip)

    pl.semaphore_wait(barrier, count - 1 + has_above.astype(jnp.int32) + has_below.astype(jnp.int32))

    strip_rows = pl.ds(outer, strip)

    def lat_copy(e):
        return pltpu.make_async_remote_copy(
            src_ref=outgoing.at[e], dst_ref=lat.at[strip_rows, lane_block(me + 1)],
            send_sem=lat_send.at[e], recv_sem=lat_recv.at[me],
            device_id={"exp": e}, device_id_type=MESH)

    def own_lat():
        return pltpu.make_async_copy(
            outgoing.at[me], lat.at[strip_rows, lane_block(me + 1)], lat_recv.at[me])

    def halo_copies(c, side):
        cols = chunk_cols(c)
        source = pl.ds(0 if side == 0 else strip - inner, inner)
        target = pl.ds(inner + strip if side == 0 else 0, inner)
        return pltpu.make_async_remote_copy(
            src_ref=coef_hbm.at[:, source, cols], dst_ref=coef.at[:, target, cols],
            send_sem=halo_send.at[side, c], recv_sem=halo_recv.at[side, c],
            device_id={"row": row - 1 if side == 0 else row + 1}, device_id_type=MESH)

    def seen_copies(side):
        source = 0 if side == 0 else strip - inner
        target = pl.ds(inner + strip if side == 0 else 0, inner)
        return [pltpu.make_async_remote_copy(
            src_ref=src.at[pl.ds(first + source, inner)], dst_ref=dst.at[target],
            send_sem=halo_send.at[side, chunks + i], recv_sem=halo_recv.at[side, chunks + i],
            device_id={"row": row - 1 if side == 0 else row + 1}, device_id_type=MESH)
            for i, (src, first, dst) in enumerate(((obs_hbm, 0, seen), (usable, inner, usable)))]

    def rim_copy(b, side):
        cols = lane_block(b + 1)
        source = pl.ds(outer if side == 0 else strip, outer)
        target = pl.ds(outer + strip if side == 0 else 0, outer)
        return pltpu.make_async_remote_copy(
            src_ref=lat.at[source, cols], dst_ref=lat.at[target, cols],
            send_sem=rim_send.at[side, b], recv_sem=rim_recv.at[side, b],
            device_id={"row": row - 1 if side == 0 else row + 1}, device_id_type=MESH)

    sends = ((0, has_above), (1, has_below))
    receives = ((0, has_below), (1, has_above))

    def start_halos(step):
        for side, there in sends:
            @pl.when(there)
            def _():
                halo_copies(ordered(step, chunks), side).start()

    late = ordered(me, count) < count // 4
    own_lat().start()
    for rank in range(count):
        e = ordered(rank, count)
        @pl.when(jnp.logical_and(e != me, jnp.logical_or(jnp.logical_not(late), rank < count // 2)))
        def _():
            lat_copy(e).start()
    start_halos(0)
    for side, there in sends:
        @pl.when(there)
        def _():
            for copy in seen_copies(side):
                copy.start()

    low_a = strip + 2 * outer - WINDOW
    low_b = strip + 2 * inner - WINDOW
    shift = LANES // 2 + half_width

    at_tap = lax.broadcasted_iota(jnp.int32, (tap_count, WINDOW), 0)
    at_lane = lax.broadcasted_iota(jnp.int32, (tap_count, WINDOW), 1)
    keep = (at_tap == at_lane).astype(jnp.float32).astype(jnp.bfloat16)
    turn = (at_tap + at_lane == tap_count - 1).astype(jnp.float32).astype(jnp.bfloat16)
    for i, (taps, order) in enumerate(((along_ref, keep), (along_ref, turn), (down_ref, keep), (down_ref, turn))):
        taps_ref[i] = jnp.dot(taps[...], order, preferred_element_type=jnp.float32)

    far = (
        lax.broadcasted_iota(jnp.int32, (WINDOW, WINDOW), 0)
        - lax.broadcasted_iota(jnp.int32, (WINDOW, WINDOW), 1))
    corner = jnp.abs(far) >= LANES

    @pl.loop(0, kernels // 2)
    def _(pair):
        for odd in range(2):
            k = 2 * pair + odd
            along = taps_ref[0, pl.ds(k, 1), :]
            along_rev = taps_ref[1, pl.ds(k, 1), :]
            down = taps_ref[2, pl.ds(k, 1), :]
            down_rev = taps_ref[3, pl.ds(k, 1), :]
            fw[pair, :, pl.ds(odd * LANES, LANES)] = toeplitz(along_rev, WINDOW, -shift)[:, :LANES].astype(fw.dtype)
            ring = toeplitz(along, WINDOW, -half_width)
            gw[k] = jnp.where(corner, 0.0, ring).astype(gw.dtype)
            reach = jnp.where(corner, ring, 0.0)
            reach = reach[:, :LANES] + reach[:, LANES:]
            ew[pair, pl.ds(odd * LANES, LANES // 2), :] = reach[:LANES // 2].astype(ew.dtype)
            ew[pair, pl.ds(odd * LANES + LANES // 2, LANES // 2), :] = reach[WINDOW - LANES // 2:].astype(ew.dtype)
            aw[k, 0] = toeplitz(down, block, outer - inner - half_width).astype(aw.dtype)
            aw[k, 1] = toeplitz(down, block, half + outer - half_width - low_a).astype(aw.dtype)
            bw[k, 0] = toeplitz(down_rev, half, inner - half_width).astype(bw.dtype)
            bw[k, 1] = toeplitz(down_rev, half, half + inner - half_width - low_b).astype(bw.dtype)

    for at in (0, chunks + 1):
        stray[at] = jnp.zeros((strip, LANES), stray.dtype)

    def take_block(rank):
        b = ordered(rank, count)
        pltpu.make_async_copy(
            outgoing.at[0], lat.at[strip_rows, lane_block(b + 1)], lat_recv.at[b]).wait()
        for side, there in sends:
            @pl.when(there)
            def _():
                rim_copy(b, side).start()

    def take_rims(rank):
        b = ordered(rank, count)
        for side, there in receives:
            @pl.when(there)
            def _():
                rim_copy(b, side).wait_recv()

    for rank in range(count // 2, count):
        @pl.when(late)
        def _():
            lat_copy(ordered(rank, count)).start()
    for rank in range(per + 1):
        take_block(rank)
    own_seen.wait()
    for side, there in receives:
        @pl.when(there)
        def _():
            for copy in seen_copies(side):
                copy.wait_recv()
    take_rims(0)

    @pl.loop(0, chunks)
    def _(step):
        c = ordered(step, chunks)
        cols = chunk_cols(c)

        @pl.when(step + 1 < chunks)
        def _():
            start_halos(step + 1)

        for more in range(1, per + 1):
            @pl.when(step * per + more < count)
            def _():
                take_rims(step * per + more)
        near = lat[:, pl.ds(pl.multiple_of(c * WINDOW, WINDOW), WINDOW + 2 * LANES)]
        lsh[...] = near[:, LANES // 2:LANES // 2 + WINDOW + LANES]
        for b in range(per):
            window = lsh[:, pl.ds(b * LANES, WINDOW)]
            for pair in range(kernels // 2):
                both = jnp.dot(window, fw[pair], preferred_element_type=jnp.float32).astype(rb.dtype)
                rb[2 * pair, :, pl.ds(b * LANES, LANES)] = both[:, :LANES]
                rb[2 * pair + 1, :, pl.ds(b * LANES, LANES)] = both[:, LANES:]
        own_coef(c).wait()
        for side, there in receives:
            @pl.when(there)
            def _():
                halo_copies(c, side).wait_recv()
        for part in range(2):
            if part == 1:
                for more in range(1, per + 1):
                    @pl.when((step + 1) * per + more < count)
                    def _():
                        take_block((step + 1) * per + more)
            rows = pl.ds(part * block, block)
            reach = pl.ds(part * low_a, WINDOW)
            predicted = jnp.zeros((block, WINDOW), jnp.float32)
            for k in range(kernels):
                vertical = jnp.dot(aw[k, part], rb[k, reach, :], preferred_element_type=jnp.float32)
                predicted += coef[k, rows, cols].astype(jnp.float32) * vertical
            mask = usable[rows, :].astype(jnp.float32)
            mask = jnp.concatenate([mask] * per, axis=1)
            resid[rows, cols] = mask * (predicted - seen[rows, cols].astype(jnp.float32))
        res_ref[:, cols] = resid[pl.ds(inner, strip), cols]

    def term_copy(b):
        return pltpu.make_async_remote_copy(
            src_ref=leaving.at[b], dst_ref=arrived.at[me],
            send_sem=term_send.at[b], recv_sem=term_recv.at[me],
            device_id={"exp": b}, device_id_type=MESH)

    lane_side = lax.broadcasted_iota(jnp.int32, (strip, LANES), 1) // (LANES // 2)

    def send_term(rank):
        b = reversed_order(rank, count)
        c, side = b // per, b % per
        beside = stray[jnp.where(side == 0, c, c + 2)]
        term = tot[:, lane_block(b)] + jnp.where(lane_side == side, beside, 0.0)
        leaving[b] = term.astype(leaving.dtype)

        @pl.when(b != me)
        def _():
            term_copy(b).start()

    @pl.loop(0, chunks)
    def _(step):
        c = reversed_order(step, chunks)
        cols = chunk_cols(c)
        inside = jnp.zeros((strip, WINDOW), jnp.float32)
        outside = jnp.zeros((strip, LANES), jnp.float32)
        left = lax.broadcasted_iota(jnp.int32, (strip, LANES), 1) < LANES // 2
        for pair in range(kernels // 2):
            edges = []
            for odd in range(2):
                k = 2 * pair + odd
                weighted = (coef[k, :, cols].astype(jnp.float32) * resid[:, cols]).astype(jnp.bfloat16)
                back = jnp.concatenate([
                    jnp.dot(
                        bw[k, part], weighted[part * low_b:part * low_b + WINDOW],
                        preferred_element_type=jnp.float32).astype(jnp.bfloat16)
                    for part in range(2)], axis=0)
                inside += jnp.dot(back, gw[k], preferred_element_type=jnp.float32)
                edges.append(jnp.where(left, back[:, :LANES], back[:, LANES:]))
            outside += jnp.dot(
                jnp.concatenate(edges, axis=1), ew[pair], preferred_element_type=jnp.float32)
        tot[:, cols] = inside
        stray[c + 1] = outside

        @pl.when(step > 0)
        def _():
            send_term(step * per - 1)

        send_term(step * per)

    send_term(count - 1)

    for c in range(grad_ref.shape[0]):
        grad_ref[c] = jnp.where(owned(me, c), leaving[me].astype(jnp.float32), 0.0)
    for rank in range(count):
        e = reversed_order(rank, count)

        @pl.when(e != me)
        def _():
            pltpu.make_async_copy(leaving.at[0], arrived.at[e], term_recv.at[e]).wait()
            value = arrived[e].astype(jnp.float32)
            for c in range(grad_ref.shape[0]):
                grad_ref[c] += jnp.where(owned(e, c), value, 0.0)

    for e in range(count):
        @pl.when(e != me)
        def _():
            lat_copy(e).wait_send()
            term_copy(e).wait_send()
    for side, there in sends:
        @pl.when(there)
        def _():
            for copy in seen_copies(side):
                copy.wait_send()
            for c in range(chunks):
                halo_copies(c, side).wait_send()
            for b in range(count):
                rim_copy(b, side).wait_send()


def fused_body(latent, row_taps, column_taps, coefficients, observed, cell_of, valid_rows):
    kernels, tap_count = row_taps.shape
    half_width = tap_count // 2
    strip, width = observed.shape[1:]
    ncells = latent.shape[0]
    inner = round_up(half_width, PACK)
    outer = round_up(2 * half_width, PACK)
    count, row_count = lax.axis_size("exp"), lax.axis_size("row")

    vmem = pl.BlockSpec(memory_space=pltpu.VMEM)
    hbm = pl.BlockSpec(memory_space=pltpu.HBM)
    chunks = width // WINDOW
    block = strip // 2 + inner
    bf16 = jnp.bfloat16
    dma = pltpu.SemaphoreType.DMA
    dims = (count, row_count, kernels, tap_count, strip, width, inner, outer)
    residual, gradient = pl.pallas_call(
        functools.partial(fused_kernel, dims),
        out_shape=(
            jax.ShapeDtypeStruct((strip, width), jnp.float32),
            jax.ShapeDtypeStruct((ncells, strip, LANES), jnp.float32),
        ),
        in_specs=[hbm] * 7,
        out_specs=(vmem, vmem),
        scratch_shapes=[
            pltpu.VMEM((1, count), jnp.int32),
            pltpu.VMEM((ncells, strip, LANES), bf16),
            pltpu.VMEM((kernels, tap_count), bf16),
            pltpu.VMEM((kernels, tap_count), bf16),
            pltpu.VMEM((1, strip), jnp.int32),
            pltpu.VMEM((count, 8, LANES), jnp.int32),
            pltpu.VMEM((4, kernels, WINDOW), jnp.float32),
            pltpu.VMEM((kernels, strip + 2 * inner, width), bf16),
            pltpu.VMEM((strip + 2 * inner, width), bf16),
            pltpu.VMEM((strip + 2 * inner, LANES), bf16),
            pltpu.VMEM((count, strip, LANES), bf16),
            pltpu.VMEM((strip + 2 * outer, width + 2 * LANES), bf16),
            pltpu.VMEM((strip + 2 * outer, WINDOW + LANES), bf16),
            pltpu.VMEM((kernels // 2, WINDOW, 2 * LANES), bf16),
            pltpu.VMEM((kernels, WINDOW, WINDOW), bf16),
            pltpu.VMEM((kernels // 2, WINDOW, LANES), bf16),
            pltpu.VMEM((kernels, 2, block, WINDOW), bf16),
            pltpu.VMEM((kernels, 2, strip // 2, WINDOW), bf16),
            pltpu.VMEM((kernels, strip + 2 * outer, WINDOW), bf16),
            pltpu.VMEM((strip + 2 * inner, width), jnp.float32),
            pltpu.VMEM((strip, width), jnp.float32),
            pltpu.VMEM((chunks + 2, strip, LANES), jnp.float32),
            pltpu.VMEM((count, strip, LANES), bf16),
            pltpu.VMEM((count, strip, LANES), bf16),
            dma((chunks + 6,)),
            dma((count,)), dma((count,)),
            dma((2, count)), dma((2, count)),
            dma((2, chunks + 2)), dma((2, chunks + 2)),
            dma((count,)), dma((count,)),
        ],
        compiler_params=pltpu.CompilerParams(
            vmem_limit_bytes=44 * 2**20, collective_id=0, has_side_effects=True),
        cost_estimate=pl.CostEstimate(flops=10**10, bytes_accessed=2 * 10**7, transcendentals=0),
    )(*[pltpu.with_memory_space_constraint(x, pltpu.HBM) for x in (
        cell_of.reshape(1, count), latent, row_taps, column_taps, valid_rows, observed[0], coefficients[0])])
    return (gradient, residual[None])


def body(latent, *others):
    if latent.shape[2] == LANES:
        return fused_body(latent, *others)
    return apart_body(latent, *others)


def solution(mesh):
    placed = (
        P(None, "row", "exp"),
        P(),
        P(),
        P("exp", None, "row", None),
        P("exp", "row", None),
        P(),
        P("exp", "row"),
    )
    return jax.shard_map(
        body,
        mesh=mesh,
        in_specs=placed,
        out_specs=(P(None, "row", "exp"), P("exp", "row", None)),
        check_vma=False,
    )
```

```python
import functools

import jax
import jax.numpy as jnp
from jax import lax
from jax.experimental import pallas as pl
from jax.experimental.pallas import tpu as pltpu
from jax.sharding import PartitionSpec as P

LANES = 128
WINDOW = 256
PACK = 16
STEP = 64
GROUP = 4
MESH = pl.DeviceIdType.MESH


def round_up(value, step):
    return -(-value // step) * step


def from_behind(block, axis, distance):
    devices = range(lax.axis_size(axis))
    route = [(i - distance, i) for i in devices if i - distance in devices]
    return lax.ppermute(block, axis, route)


def toeplitz(taps_row, rows, first):
    parts = []
    for at in range(0, rows, STEP):
        moved = pltpu.roll(jnp.broadcast_to(taps_row, (8, WINDOW)), (first + at) % WINDOW, 1)
        spread = jnp.broadcast_to(moved[:1], (min(STEP, rows - at), WINDOW))
        parts.append(pltpu.roll(spread, 0, 1, stride=1, stride_axis=0))
    return jnp.concatenate(parts, axis=0)


def filters_kernel(
    dims,
    lat_ref, taps_ref, obs_ref, mask_ref, coef_hbm, above_hbm, below_hbm,
    res_ref, term_ref,
    coef, lsh, fw, gw, aw, bw, rb, resid, cb, tsh, sems,
):
    kernels, tap_count, strip, width, inner, outer = dims
    half_width = tap_count // 2
    half = strip // 2
    block = half + inner
    chunks = width // WINDOW

    def copies(c):
        cols = pl.ds(c * WINDOW, WINDOW)
        return (
            pltpu.make_async_copy(
                coef_hbm.at[:, :, cols], coef.at[:, pl.ds(inner, strip), cols], sems.at[c, 0]),
            pltpu.make_async_copy(
                above_hbm.at[:, :, cols], coef.at[:, pl.ds(0, inner), cols], sems.at[c, 1]),
            pltpu.make_async_copy(
                below_hbm.at[:, :, cols], coef.at[:, pl.ds(inner + strip, inner), cols], sems.at[c, 2]),
        )

    for c in range(chunks):
        for copy in copies(c):
            copy.start()

    lsh[:, pl.ds(0, LANES)] = jnp.zeros((lsh.shape[0], LANES), lsh.dtype)
    lsh[:, pl.ds(width, LANES)] = jnp.zeros((lsh.shape[0], LANES), lsh.dtype)
    lsh[:, pl.ds(LANES // 2, width)] = lat_ref[...]

    low_a = strip + 2 * outer - WINDOW
    low_b = strip + 2 * inner - WINDOW
    side = LANES // 2 + half_width

    @pl.loop(0, kernels // 2)
    def _(pair):
        for odd in range(2):
            k = 2 * pair + odd
            row = taps_ref[0, pl.ds(k, 1), :]
            row_rev = taps_ref[1, pl.ds(k, 1), :]
            col = taps_ref[2, pl.ds(k, 1), :]
            col_rev = taps_ref[3, pl.ds(k, 1), :]
            shape = (pl.ds(odd * LANES, LANES))
            fw[pair, :, shape] = toeplitz(row_rev, WINDOW, -side)[:, :LANES].astype(fw.dtype)
            gw[k] = toeplitz(row, WINDOW, -side)[:, :LANES].astype(gw.dtype)
            aw[k, 0] = toeplitz(col, block, outer - inner - half_width).astype(aw.dtype)
            aw[k, 1] = toeplitz(col, block, half + outer - half_width - low_a).astype(aw.dtype)
            bw[k, 0] = toeplitz(col_rev, half, inner - half_width).astype(bw.dtype)
            bw[k, 1] = toeplitz(col_rev, half, half + inner - half_width - low_b).astype(bw.dtype)

    @pl.loop(0, chunks)
    def _(c):
        for copy in copies(c):
            copy.wait()
        start = pl.multiple_of(c * WINDOW, WINDOW)
        cols = pl.ds(start, WINDOW)
        for b in range(WINDOW // LANES):
            window = lsh[:, pl.ds(pl.multiple_of(start + b * LANES, LANES), WINDOW)]
            for pair in range(kernels // 2):
                both = jnp.dot(window, fw[pair], preferred_element_type=jnp.float32).astype(rb.dtype)
                rb[2 * pair, :, pl.ds(b * LANES, LANES)] = both[:, :LANES]
                rb[2 * pair + 1, :, pl.ds(b * LANES, LANES)] = both[:, LANES:]
        for part in range(2):
            rows = pl.ds(part * block, block)
            seen = pl.ds(part * low_a, WINDOW)
            predicted = jnp.zeros((block, WINDOW), jnp.float32)
            for k in range(kernels):
                vertical = jnp.dot(aw[k, part], rb[k, seen, :], preferred_element_type=jnp.float32)
                predicted += coef[k, rows, cols].astype(jnp.float32) * vertical
            mask = mask_ref[rows, :]
            mask = jnp.concatenate([mask] * (WINDOW // LANES), axis=1)
            resid[rows, :] = mask * (predicted - obs_ref[rows, cols].astype(jnp.float32))
        res_ref[:, cols] = resid[pl.ds(inner, strip), :]
        for k in range(kernels):
            weighted = (coef[k, :, cols].astype(jnp.float32) * resid[...]).astype(jnp.bfloat16)
            for part in range(2):
                seen = weighted[part * low_b:part * low_b + WINDOW]
                back = jnp.dot(bw[k, part], seen, preferred_element_type=jnp.float32)
                cb[k, pl.ds(part * half, half), cols] = back.astype(cb.dtype)

    blocks = width // LANES
    for out, source, taps_at in (
        (0, 0, LANES), (width, width - LANES, 0),
    ):
        total = jnp.zeros((strip, LANES), jnp.float32)
        for k in range(kernels):
            total += jnp.dot(
                cb[k, :, pl.ds(source, LANES)], gw[k, pl.ds(taps_at, LANES), :],
                preferred_element_type=jnp.float32)
        tsh[:, pl.ds(out, LANES)] = total

    @pl.loop(0, blocks - 1)
    def _(b):
        source = pl.multiple_of(b * LANES, LANES)
        total = jnp.zeros((strip, LANES), jnp.float32)
        for k in range(kernels):
            total += jnp.dot(
                cb[k, :, pl.ds(source, WINDOW)], gw[k], preferred_element_type=jnp.float32)
        tsh[:, pl.ds(pl.multiple_of(source + LANES, LANES), LANES)] = total

    term_ref[...] = tsh[:, pl.ds(LANES // 2, width)].astype(term_ref.dtype)


def apart_body(latent, row_taps, column_taps, coefficients, observed, cell_of, valid_rows):
    kernels, tap_count = row_taps.shape
    half_width = tap_count // 2
    strip, width = observed.shape[1:]
    ncells = latent.shape[0]
    inner = round_up(half_width, PACK)
    outer = round_up(2 * half_width, PACK)
    cell_list = cell_of[:, 0]

    above_coef = from_behind(coefficients[0, :, strip - inner:], "row", 1)
    below_coef = from_behind(coefficients[0, :, :inner], "row", -1)
    usable = jnp.broadcast_to(valid_rows[0].astype(jnp.bfloat16)[:, None], (strip, LANES))
    seen = jnp.concatenate([observed[0], usable], axis=1)
    seen = jnp.concatenate(
        [from_behind(seen[strip - inner:], "row", 1), seen, from_behind(seen[:inner], "row", -1)], axis=0)
    mask = seen[:, width:].astype(jnp.float32)
    seen = seen[:, :width]

    outgoing = jnp.take(latent, cell_list, axis=0)
    arrived = lax.all_to_all(outgoing, "exp", split_axis=0, concat_axis=2, tiled=True)[0]
    extended = jnp.concatenate(
        [from_behind(arrived[strip - outer:], "row", 1), arrived, from_behind(arrived[:outer], "row", -1)], axis=0)

    taps = jnp.stack([row_taps, row_taps[:, ::-1], column_taps, column_taps[:, ::-1]]).astype(jnp.float32)
    taps = jnp.pad(taps, ((0, 0), (0, 0), (0, WINDOW - tap_count)))

    vmem = pl.BlockSpec(memory_space=pltpu.VMEM)
    hbm = pl.BlockSpec(memory_space=pl.ANY)
    dims = (kernels, tap_count, strip, width, inner, outer)
    block = strip // 2 + inner
    bf16 = jnp.bfloat16
    residual, term = pl.pallas_call(
        functools.partial(filters_kernel, dims),
        out_shape=(
            jax.ShapeDtypeStruct((strip, width), jnp.float32),
            jax.ShapeDtypeStruct((strip, width), bf16),
        ),
        in_specs=[vmem, vmem, vmem, vmem, hbm, hbm, hbm],
        out_specs=(vmem, vmem),
        scratch_shapes=[
            pltpu.VMEM((kernels, strip + 2 * inner, width), bf16),
            pltpu.VMEM((strip + 2 * outer, width + LANES), bf16),
            pltpu.VMEM((kernels // 2, WINDOW, 2 * LANES), bf16),
            pltpu.VMEM((kernels, WINDOW, LANES), bf16),
            pltpu.VMEM((kernels, 2, block, WINDOW), bf16),
            pltpu.VMEM((kernels, 2, strip // 2, WINDOW), bf16),
            pltpu.VMEM((kernels, strip + 2 * outer, WINDOW), bf16),
            pltpu.VMEM((strip + 2 * inner, WINDOW), jnp.float32),
            pltpu.VMEM((kernels, strip, width), bf16),
            pltpu.VMEM((strip, width + LANES), jnp.float32),
            pltpu.SemaphoreType.DMA((width // WINDOW, 3)),
        ],
        compiler_params=pltpu.CompilerParams(vmem_limit_bytes=56 * 2**20),
        cost_estimate=pl.CostEstimate(flops=10**10, bytes_accessed=2 * 10**7, transcendentals=0),
    )(extended, taps, seen, mask, coefficients[0], above_coef, below_coef)

    incoming = lax.all_to_all(term[None], "exp", split_axis=2, concat_axis=0, tiled=True)
    owner = jnp.arange(ncells)[:, None] == cell_list[None, :]
    gradient = jnp.sum(
        jnp.where(owner[:, :, None, None], incoming[None].astype(jnp.float32), 0.0), axis=1)
    return (gradient, residual[None])


def fused_kernel(
    dims,
    cells_hbm, lat_hbm, along_hbm, down_hbm, valid_hbm, obs_hbm, coef_hbm,
    res_ref, grad_ref,
    cells_ref, lat_ref, along_ref, down_ref, valid_ref, cells, taps_ref, coef, seen, usable, outgoing, lat, lsh, fw, gw, ew, aw, bw, rb, resid, tot, stray, leaving, arrived,
    own_sems, lat_send, lat_recv, rim_send, rim_recv, halo_send, halo_recv, term_send, term_recv,
):
    count, row_count, kernels, tap_count, strip, width, inner, outer = dims
    half_width = tap_count // 2
    half = strip // 2
    block = half + inner
    chunks = width // WINDOW
    per = WINDOW // LANES
    me = lax.axis_index("exp")
    row = lax.axis_index("row")
    rising = me < count // 2
    has_above = row > 0
    has_below = row < row_count - 1

    def ordered(rank, length):
        return jnp.where(rising, rank, length - 1 - rank)

    def reversed_order(rank, length):
        return jnp.where(rising, length - 1 - rank, rank)

    def lane_block(b):
        return pl.ds(pl.multiple_of(b * LANES, LANES), LANES)

    def chunk_cols(c):
        return pl.ds(pl.multiple_of(c * WINDOW, WINDOW), WINDOW)

    barrier = pltpu.get_barrier_semaphore()
    for e in range(count):
        @pl.when(e != me)
        def _():
            pl.semaphore_signal(barrier, inc=1, device_id={"exp": e}, device_id_type=MESH)

    @pl.when(has_above)
    def _():
        pl.semaphore_signal(barrier, inc=1, device_id={"row": row - 1}, device_id_type=MESH)

    @pl.when(has_below)
    def _():
        pl.semaphore_signal(barrier, inc=1, device_id={"row": row + 1}, device_id_type=MESH)

    def own_coef(c):
        cols = chunk_cols(c)
        return pltpu.make_async_copy(
            coef_hbm.at[:, :, cols], coef.at[:, pl.ds(inner, strip), cols], own_sems.at[c])

    own_seen = pltpu.make_async_copy(obs_hbm, seen.at[pl.ds(inner, strip)], own_sems.at[chunks])
    fetched = [
        pltpu.make_async_copy(src, dst, own_sems.at[chunks + 1 + i])
        for i, (src, dst) in enumerate((
            (cells_hbm, cells_ref), (lat_hbm, lat_ref), (along_hbm, along_ref),
            (down_hbm, down_ref), (valid_hbm, valid_ref)))]
    for copy in fetched:
        copy.start()
    own_seen.start()
    for step in range(chunks):
        own_coef(ordered(step, chunks)).start()

    for copy in fetched:
        copy.wait()
    for e in range(count):
        cells[e] = jnp.broadcast_to(cells_ref[:, e:e + 1], (8, LANES))

    def owned(e, c):
        return jnp.concatenate([(cells[e] == c).astype(jnp.float32)] * (strip // 8), axis=0) > 0.5

    for e in range(count):
        chosen = lat_ref[0].astype(jnp.float32)
        for c in range(1, lat_ref.shape[0]):
            chosen = jnp.where(owned(e, c), lat_ref[c].astype(jnp.float32), chosen)
        outgoing[e] = chosen.astype(outgoing.dtype)
    at_row = lax.broadcasted_iota(jnp.int32, (strip, strip), 0)
    at_col = lax.broadcasted_iota(jnp.int32, (strip, strip), 1)
    spread = jnp.where(at_row == at_col, valid_ref[...], 0).astype(jnp.bfloat16)
    usable[pl.ds(inner, strip), :] = jnp.dot(
        spread, jnp.ones((strip, LANES), jnp.bfloat16),
        preferred_element_type=jnp.float32).astype(usable.dtype)
    for ref in (lat,):
        ref[:, pl.ds(0, LANES)] = jnp.zeros((ref.shape[0], LANES), ref.dtype)
        ref[:, pl.ds(LANES + width, LANES)] = jnp.zeros((ref.shape[0], LANES), ref.dtype)

    def fill(at_lat, at_inner):
        lat[pl.ds(at_lat, outer), :] = jnp.zeros((outer, lat.shape[1]), lat.dtype)
        coef[:, pl.ds(at_inner, inner), :] = jnp.zeros((kernels, inner, width), coef.dtype)
        seen[pl.ds(at_inner, inner), :] = jnp.zeros((inner, width), seen.dtype)
        usable[pl.ds(at_inner, inner), :] = jnp.zeros((inner, LANES), usable.dtype)

    @pl.when(jnp.logical_not(has_above))
    def _():
        fill(0, 0)

    @pl.when(jnp.logical_not(has_below))
    def _():
        fill(outer + strip, inner + strip)

    pl.semaphore_wait(barrier, count - 1 + has_above.astype(jnp.int32) + has_below.astype(jnp.int32))

    strip_rows = pl.ds(outer, strip)

    def lat_copy(e):
        return pltpu.make_async_remote_copy(
            src_ref=outgoing.at[e], dst_ref=lat.at[strip_rows, lane_block(me + 1)],
            send_sem=lat_send.at[e], recv_sem=lat_recv.at[me],
            device_id={"exp": e}, device_id_type=MESH)

    def own_lat():
        return pltpu.make_async_copy(
            outgoing.at[me], lat.at[strip_rows, lane_block(me + 1)], lat_recv.at[me])

    def halo_copies(c, side):
        cols = chunk_cols(c)
        source = pl.ds(0 if side == 0 else strip - inner, inner)
        target = pl.ds(inner + strip if side == 0 else 0, inner)
        return pltpu.make_async_remote_copy(
            src_ref=coef_hbm.at[:, source, cols], dst_ref=coef.at[:, target, cols],
            send_sem=halo_send.at[side, c], recv_sem=halo_recv.at[side, c],
            device_id={"row": row - 1 if side == 0 else row + 1}, device_id_type=MESH)

    def seen_copies(side):
        source = 0 if side == 0 else strip - inner
        target = pl.ds(inner + strip if side == 0 else 0, inner)
        return [pltpu.make_async_remote_copy(
            src_ref=src.at[pl.ds(first + source, inner)], dst_ref=dst.at[target],
            send_sem=halo_send.at[side, chunks + i], recv_sem=halo_recv.at[side, chunks + i],
            device_id={"row": row - 1 if side == 0 else row + 1}, device_id_type=MESH)
            for i, (src, first, dst) in enumerate(((obs_hbm, 0, seen), (usable, inner, usable)))]

    def rim_copy(b, side):
        cols = lane_block(b + 1)
        source = pl.ds(outer if side == 0 else strip, outer)
        target = pl.ds(outer + strip if side == 0 else 0, outer)
        return pltpu.make_async_remote_copy(
            src_ref=lat.at[source, cols], dst_ref=lat.at[target, cols],
            send_sem=rim_send.at[side, b], recv_sem=rim_recv.at[side, b],
            device_id={"row": row - 1 if side == 0 else row + 1}, device_id_type=MESH)

    sends = ((0, has_above), (1, has_below))
    receives = ((0, has_below), (1, has_above))

    def start_halos(step):
        for side, there in sends:
            @pl.when(there)
            def _():
                halo_copies(ordered(step, chunks), side).start()

    late = ordered(me, count) < count // 4
    own_lat().start()
    for rank in range(count):
        e = ordered(rank, count)
        @pl.when(jnp.logical_and(e != me, jnp.logical_or(jnp.logical_not(late), rank < count // 2)))
        def _():
            lat_copy(e).start()
    start_halos(0)
    for side, there in sends:
        @pl.when(there)
        def _():
            for copy in seen_copies(side):
                copy.start()

    low_a = strip + 2 * outer - WINDOW
    low_b = strip + 2 * inner - WINDOW
    shift = LANES // 2 + half_width

    at_tap = lax.broadcasted_iota(jnp.int32, (tap_count, WINDOW), 0)
    at_lane = lax.broadcasted_iota(jnp.int32, (tap_count, WINDOW), 1)
    keep = (at_tap == at_lane).astype(jnp.float32).astype(jnp.bfloat16)
    turn = (at_tap + at_lane == tap_count - 1).astype(jnp.float32).astype(jnp.bfloat16)
    for i, (taps, order) in enumerate(((along_ref, keep), (along_ref, turn), (down_ref, keep), (down_ref, turn))):
        taps_ref[i] = jnp.dot(taps[...], order, preferred_element_type=jnp.float32)

    far = (
        lax.broadcasted_iota(jnp.int32, (WINDOW, WINDOW), 0)
        - lax.broadcasted_iota(jnp.int32, (WINDOW, WINDOW), 1))
    corner = jnp.abs(far) >= LANES

    @pl.loop(0, kernels // 2)
    def _(pair):
        for odd in range(2):
            k = 2 * pair + odd
            along = taps_ref[0, pl.ds(k, 1), :]
            along_rev = taps_ref[1, pl.ds(k, 1), :]
            down = taps_ref[2, pl.ds(k, 1), :]
            down_rev = taps_ref[3, pl.ds(k, 1), :]
            fw[pair, :, pl.ds(odd * LANES, LANES)] = toeplitz(along_rev, WINDOW, -shift)[:, :LANES].astype(fw.dtype)
            ring = toeplitz(along, WINDOW, -half_width)
            gw[k] = jnp.where(corner, 0.0, ring).astype(gw.dtype)
            reach = jnp.where(corner, ring, 0.0)
            reach = reach[:, :LANES] + reach[:, LANES:]
            ew[pair, pl.ds(odd * LANES, LANES // 2), :] = reach[:LANES // 2].astype(ew.dtype)
            ew[pair, pl.ds(odd * LANES + LANES // 2, LANES // 2), :] = reach[WINDOW - LANES // 2:].astype(ew.dtype)
            aw[k, 0] = toeplitz(down, block, outer - inner - half_width).astype(aw.dtype)
            aw[k, 1] = toeplitz(down, block, half + outer - half_width - low_a).astype(aw.dtype)
            bw[k, 0] = toeplitz(down_rev, half, inner - half_width).astype(bw.dtype)
            bw[k, 1] = toeplitz(down_rev, half, half + inner - half_width - low_b).astype(bw.dtype)

    for at in (0, chunks + 1):
        stray[at] = jnp.zeros((strip, LANES), stray.dtype)

    def take_block(rank):
        b = ordered(rank, count)
        pltpu.make_async_copy(
            outgoing.at[0], lat.at[strip_rows, lane_block(b + 1)], lat_recv.at[b]).wait()
        for side, there in sends:
            @pl.when(there)
            def _():
                rim_copy(b, side).start()

    def take_rims(rank):
        b = ordered(rank, count)
        for side, there in receives:
            @pl.when(there)
            def _():
                rim_copy(b, side).wait_recv()

    for rank in range(count // 2, count):
        @pl.when(late)
        def _():
            lat_copy(ordered(rank, count)).start()
    for rank in range(per + 1):
        take_block(rank)
    own_seen.wait()
    for side, there in receives:
        @pl.when(there)
        def _():
            for copy in seen_copies(side):
                copy.wait_recv()
    take_rims(0)

    @pl.loop(0, chunks)
    def _(step):
        c = ordered(step, chunks)
        cols = chunk_cols(c)

        @pl.when(step + 1 < chunks)
        def _():
            start_halos(step + 1)

        for more in range(1, per + 1):
            @pl.when(step * per + more < count)
            def _():
                take_rims(step * per + more)
        near = lat[:, pl.ds(pl.multiple_of(c * WINDOW, WINDOW), WINDOW + 2 * LANES)]
        lsh[...] = near[:, LANES // 2:LANES // 2 + WINDOW + LANES]
        for b in range(per):
            window = lsh[:, pl.ds(b * LANES, WINDOW)]
            for pair in range(kernels // 2):
                both = jnp.dot(window, fw[pair], preferred_element_type=jnp.float32).astype(rb.dtype)
                rb[2 * pair, :, pl.ds(b * LANES, LANES)] = both[:, :LANES]
                rb[2 * pair + 1, :, pl.ds(b * LANES, LANES)] = both[:, LANES:]
        own_coef(c).wait()
        for side, there in receives:
            @pl.when(there)
            def _():
                halo_copies(c, side).wait_recv()
        for part in range(2):
            if part == 1:
                for more in range(1, per + 1):
                    @pl.when((step + 1) * per + more < count)
                    def _():
                        take_block((step + 1) * per + more)
            rows = pl.ds(part * block, block)
            reach = pl.ds(part * low_a, WINDOW)
            predicted = jnp.zeros((block, WINDOW), jnp.float32)
            for k in range(kernels):
                vertical = jnp.dot(aw[k, part], rb[k, reach, :], preferred_element_type=jnp.float32)
                predicted += coef[k, rows, cols].astype(jnp.float32) * vertical
            mask = usable[rows, :].astype(jnp.float32)
            mask = jnp.concatenate([mask] * per, axis=1)
            resid[rows, cols] = mask * (predicted - seen[rows, cols].astype(jnp.float32))
        res_ref[:, cols] = resid[pl.ds(inner, strip), cols]

    def term_copy(b):
        return pltpu.make_async_remote_copy(
            src_ref=leaving.at[b], dst_ref=arrived.at[me],
            send_sem=term_send.at[b], recv_sem=term_recv.at[me],
            device_id={"exp": b}, device_id_type=MESH)

    lane_side = lax.broadcasted_iota(jnp.int32, (strip, LANES), 1) // (LANES // 2)

    def send_term(rank):
        b = reversed_order(rank, count)
        c, side = b // per, b % per
        beside = stray[jnp.where(side == 0, c, c + 2)]
        term = tot[:, lane_block(b)] + jnp.where(lane_side == side, beside, 0.0)
        leaving[b] = term.astype(leaving.dtype)

        @pl.when(b != me)
        def _():
            term_copy(b).start()

    @pl.loop(0, chunks)
    def _(step):
        c = reversed_order(step, chunks)
        cols = chunk_cols(c)
        inside = jnp.zeros((strip, WINDOW), jnp.float32)
        outside = jnp.zeros((strip, LANES), jnp.float32)
        left = lax.broadcasted_iota(jnp.int32, (strip, LANES), 1) < LANES // 2
        for group in range(kernels // GROUP):
            backs, edges = [], []
            for odd in range(GROUP):
                k = GROUP * group + odd
                weighted = (coef[k, :, cols].astype(jnp.float32) * resid[:, cols]).astype(jnp.bfloat16)
                back = jnp.concatenate([
                    jnp.dot(
                        bw[k, part], weighted[part * low_b:part * low_b + WINDOW],
                        preferred_element_type=jnp.float32).astype(jnp.bfloat16)
                    for part in range(2)], axis=0)
                backs.append(back)
                edges.append(jnp.where(left, back[:, :LANES], back[:, LANES:]))
            inside += jnp.dot(
                jnp.concatenate(backs, axis=1),
                gw[GROUP * group:GROUP * (group + 1)].reshape(GROUP * WINDOW, WINDOW),
                preferred_element_type=jnp.float32)
            outside += jnp.dot(
                jnp.concatenate(edges, axis=1),
                ew[GROUP // 2 * group:GROUP // 2 * (group + 1)].reshape(GROUP * LANES, LANES),
                preferred_element_type=jnp.float32)
        tot[:, cols] = inside
        stray[c + 1] = outside

        @pl.when(step > 0)
        def _():
            send_term(step * per - 1)

        send_term(step * per)

    send_term(count - 1)

    for c in range(grad_ref.shape[0]):
        grad_ref[c] = jnp.where(owned(me, c), leaving[me].astype(jnp.float32), 0.0)
    for rank in range(count):
        e = reversed_order(rank, count)

        @pl.when(e != me)
        def _():
            pltpu.make_async_copy(leaving.at[0], arrived.at[e], term_recv.at[e]).wait()
            value = arrived[e].astype(jnp.float32)
            for c in range(grad_ref.shape[0]):
                grad_ref[c] += jnp.where(owned(e, c), value, 0.0)

    for e in range(count):
        @pl.when(e != me)
        def _():
            lat_copy(e).wait_send()
            term_copy(e).wait_send()
    for side, there in sends:
        @pl.when(there)
        def _():
            for copy in seen_copies(side):
                copy.wait_send()
            for c in range(chunks):
                halo_copies(c, side).wait_send()
            for b in range(count):
                rim_copy(b, side).wait_send()


def fused_body(latent, row_taps, column_taps, coefficients, observed, cell_of, valid_rows):
    kernels, tap_count = row_taps.shape
    half_width = tap_count // 2
    strip, width = observed.shape[1:]
    ncells = latent.shape[0]
    inner = round_up(half_width, PACK)
    outer = round_up(2 * half_width, PACK)
    count, row_count = lax.axis_size("exp"), lax.axis_size("row")

    vmem = pl.BlockSpec(memory_space=pltpu.VMEM)
    hbm = pl.BlockSpec(memory_space=pltpu.HBM)
    chunks = width // WINDOW
    block = strip // 2 + inner
    bf16 = jnp.bfloat16
    dma = pltpu.SemaphoreType.DMA
    dims = (count, row_count, kernels, tap_count, strip, width, inner, outer)
    residual, gradient = pl.pallas_call(
        functools.partial(fused_kernel, dims),
        out_shape=(
            jax.ShapeDtypeStruct((strip, width), jnp.float32),
            jax.ShapeDtypeStruct((ncells, strip, LANES), jnp.float32),
        ),
        in_specs=[hbm] * 7,
        out_specs=(vmem, vmem),
        scratch_shapes=[
            pltpu.VMEM((1, count), jnp.int32),
            pltpu.VMEM((ncells, strip, LANES), bf16),
            pltpu.VMEM((kernels, tap_count), bf16),
            pltpu.VMEM((kernels, tap_count), bf16),
            pltpu.VMEM((1, strip), jnp.int32),
            pltpu.VMEM((count, 8, LANES), jnp.int32),
            pltpu.VMEM((4, kernels, WINDOW), jnp.float32),
            pltpu.VMEM((kernels, strip + 2 * inner, width), bf16),
            pltpu.VMEM((strip + 2 * inner, width), bf16),
            pltpu.VMEM((strip + 2 * inner, LANES), bf16),
            pltpu.VMEM((count, strip, LANES), bf16),
            pltpu.VMEM((strip + 2 * outer, width + 2 * LANES), bf16),
            pltpu.VMEM((strip + 2 * outer, WINDOW + LANES), bf16),
            pltpu.VMEM((kernels // 2, WINDOW, 2 * LANES), bf16),
            pltpu.VMEM((kernels, WINDOW, WINDOW), bf16),
            pltpu.VMEM((kernels // 2, WINDOW, LANES), bf16),
            pltpu.VMEM((kernels, 2, block, WINDOW), bf16),
            pltpu.VMEM((kernels, 2, strip // 2, WINDOW), bf16),
            pltpu.VMEM((kernels, strip + 2 * outer, WINDOW), bf16),
            pltpu.VMEM((strip + 2 * inner, width), jnp.float32),
            pltpu.VMEM((strip, width), jnp.float32),
            pltpu.VMEM((chunks + 2, strip, LANES), jnp.float32),
            pltpu.VMEM((count, strip, LANES), bf16),
            pltpu.VMEM((count, strip, LANES), bf16),
            dma((chunks + 6,)),
            dma((count,)), dma((count,)),
            dma((2, count)), dma((2, count)),
            dma((2, chunks + 2)), dma((2, chunks + 2)),
            dma((count,)), dma((count,)),
        ],
        compiler_params=pltpu.CompilerParams(
            vmem_limit_bytes=44 * 2**20, collective_id=0, has_side_effects=True),
        cost_estimate=pl.CostEstimate(flops=10**10, bytes_accessed=2 * 10**7, transcendentals=0),
    )(*[pltpu.with_memory_space_constraint(x, pltpu.HBM) for x in (
        cell_of.reshape(1, count), latent, row_taps, column_taps, valid_rows, observed[0], coefficients[0])])
    return (gradient, residual[None])


def body(latent, *others):
    if latent.shape[2] == LANES:
        return fused_body(latent, *others)
    return apart_body(latent, *others)


def solution(mesh):
    placed = (
        P(None, "row", "exp"),
        P(),
        P(),
        P("exp", None, "row", None),
        P("exp", "row", None),
        P(),
        P("exp", "row"),
    )
    return jax.shard_map(
        body,
        mesh=mesh,
        in_specs=placed,
        out_specs=(P(None, "row", "exp"), P("exp", "row", None)),
        check_vma=False,
    )
```

```python
import functools

import jax
import jax.numpy as jnp
from jax import lax
from jax.experimental import pallas as pl
from jax.experimental.pallas import tpu as pltpu
from jax.sharding import PartitionSpec as P

LANES = 128
WINDOW = 256
PACK = 16
STEP = 64
GROUP = 8
MESH = pl.DeviceIdType.MESH


def round_up(value, step):
    return -(-value // step) * step


def from_behind(block, axis, distance):
    devices = range(lax.axis_size(axis))
    route = [(i - distance, i) for i in devices if i - distance in devices]
    return lax.ppermute(block, axis, route)


def toeplitz(taps_row, rows, first):
    parts = []
    for at in range(0, rows, STEP):
        moved = pltpu.roll(jnp.broadcast_to(taps_row, (8, WINDOW)), (first + at) % WINDOW, 1)
        spread = jnp.broadcast_to(moved[:1], (min(STEP, rows - at), WINDOW))
        parts.append(pltpu.roll(spread, 0, 1, stride=1, stride_axis=0))
    return jnp.concatenate(parts, axis=0)


def filters_kernel(
    dims,
    lat_ref, taps_ref, obs_ref, mask_ref, coef_hbm, above_hbm, below_hbm,
    res_ref, term_ref,
    coef, lsh, fw, gw, aw, bw, rb, resid, cb, tsh, sems,
):
    kernels, tap_count, strip, width, inner, outer = dims
    half_width = tap_count // 2
    half = strip // 2
    block = half + inner
    chunks = width // WINDOW

    def copies(c):
        cols = pl.ds(c * WINDOW, WINDOW)
        return (
            pltpu.make_async_copy(
                coef_hbm.at[:, :, cols], coef.at[:, pl.ds(inner, strip), cols], sems.at[c, 0]),
            pltpu.make_async_copy(
                above_hbm.at[:, :, cols], coef.at[:, pl.ds(0, inner), cols], sems.at[c, 1]),
            pltpu.make_async_copy(
                below_hbm.at[:, :, cols], coef.at[:, pl.ds(inner + strip, inner), cols], sems.at[c, 2]),
        )

    for c in range(chunks):
        for copy in copies(c):
            copy.start()

    lsh[:, pl.ds(0, LANES)] = jnp.zeros((lsh.shape[0], LANES), lsh.dtype)
    lsh[:, pl.ds(width, LANES)] = jnp.zeros((lsh.shape[0], LANES), lsh.dtype)
    lsh[:, pl.ds(LANES // 2, width)] = lat_ref[...]

    low_a = strip + 2 * outer - WINDOW
    low_b = strip + 2 * inner - WINDOW
    side = LANES // 2 + half_width

    @pl.loop(0, kernels // 2)
    def _(pair):
        for odd in range(2):
            k = 2 * pair + odd
            row = taps_ref[0, pl.ds(k, 1), :]
            row_rev = taps_ref[1, pl.ds(k, 1), :]
            col = taps_ref[2, pl.ds(k, 1), :]
            col_rev = taps_ref[3, pl.ds(k, 1), :]
            shape = (pl.ds(odd * LANES, LANES))
            fw[pair, :, shape] = toeplitz(row_rev, WINDOW, -side)[:, :LANES].astype(fw.dtype)
            gw[k] = toeplitz(row, WINDOW, -side)[:, :LANES].astype(gw.dtype)
            aw[k, 0] = toeplitz(col, block, outer - inner - half_width).astype(aw.dtype)
            aw[k, 1] = toeplitz(col, block, half + outer - half_width - low_a).astype(aw.dtype)
            bw[k, 0] = toeplitz(col_rev, half, inner - half_width).astype(bw.dtype)
            bw[k, 1] = toeplitz(col_rev, half, half + inner - half_width - low_b).astype(bw.dtype)

    @pl.loop(0, chunks)
    def _(c):
        for copy in copies(c):
            copy.wait()
        start = pl.multiple_of(c * WINDOW, WINDOW)
        cols = pl.ds(start, WINDOW)
        for b in range(WINDOW // LANES):
            window = lsh[:, pl.ds(pl.multiple_of(start + b * LANES, LANES), WINDOW)]
            for pair in range(kernels // 2):
                both = jnp.dot(window, fw[pair], preferred_element_type=jnp.float32).astype(rb.dtype)
                rb[2 * pair, :, pl.ds(b * LANES, LANES)] = both[:, :LANES]
                rb[2 * pair + 1, :, pl.ds(b * LANES, LANES)] = both[:, LANES:]
        for part in range(2):
            rows = pl.ds(part * block, block)
            seen = pl.ds(part * low_a, WINDOW)
            predicted = jnp.zeros((block, WINDOW), jnp.float32)
            for k in range(kernels):
                vertical = jnp.dot(aw[k, part], rb[k, seen, :], preferred_element_type=jnp.float32)
                predicted += coef[k, rows, cols].astype(jnp.float32) * vertical
            mask = mask_ref[rows, :]
            mask = jnp.concatenate([mask] * (WINDOW // LANES), axis=1)
            resid[rows, :] = mask * (predicted - obs_ref[rows, cols].astype(jnp.float32))
        res_ref[:, cols] = resid[pl.ds(inner, strip), :]
        for k in range(kernels):
            weighted = (coef[k, :, cols].astype(jnp.float32) * resid[...]).astype(jnp.bfloat16)
            for part in range(2):
                seen = weighted[part * low_b:part * low_b + WINDOW]
                back = jnp.dot(bw[k, part], seen, preferred_element_type=jnp.float32)
                cb[k, pl.ds(part * half, half), cols] = back.astype(cb.dtype)

    blocks = width // LANES
    for out, source, taps_at in (
        (0, 0, LANES), (width, width - LANES, 0),
    ):
        total = jnp.zeros((strip, LANES), jnp.float32)
        for k in range(kernels):
            total += jnp.dot(
                cb[k, :, pl.ds(source, LANES)], gw[k, pl.ds(taps_at, LANES), :],
                preferred_element_type=jnp.float32)
        tsh[:, pl.ds(out, LANES)] = total

    @pl.loop(0, blocks - 1)
    def _(b):
        source = pl.multiple_of(b * LANES, LANES)
        total = jnp.zeros((strip, LANES), jnp.float32)
        for k in range(kernels):
            total += jnp.dot(
                cb[k, :, pl.ds(source, WINDOW)], gw[k], preferred_element_type=jnp.float32)
        tsh[:, pl.ds(pl.multiple_of(source + LANES, LANES), LANES)] = total

    term_ref[...] = tsh[:, pl.ds(LANES // 2, width)].astype(term_ref.dtype)


def apart_body(latent, row_taps, column_taps, coefficients, observed, cell_of, valid_rows):
    kernels, tap_count = row_taps.shape
    half_width = tap_count // 2
    strip, width = observed.shape[1:]
    ncells = latent.shape[0]
    inner = round_up(half_width, PACK)
    outer = round_up(2 * half_width, PACK)
    cell_list = cell_of[:, 0]

    above_coef = from_behind(coefficients[0, :, strip - inner:], "row", 1)
    below_coef = from_behind(coefficients[0, :, :inner], "row", -1)
    usable = jnp.broadcast_to(valid_rows[0].astype(jnp.bfloat16)[:, None], (strip, LANES))
    seen = jnp.concatenate([observed[0], usable], axis=1)
    seen = jnp.concatenate(
        [from_behind(seen[strip - inner:], "row", 1), seen, from_behind(seen[:inner], "row", -1)], axis=0)
    mask = seen[:, width:].astype(jnp.float32)
    seen = seen[:, :width]

    outgoing = jnp.take(latent, cell_list, axis=0)
    arrived = lax.all_to_all(outgoing, "exp", split_axis=0, concat_axis=2, tiled=True)[0]
    extended = jnp.concatenate(
        [from_behind(arrived[strip - outer:], "row", 1), arrived, from_behind(arrived[:outer], "row", -1)], axis=0)

    taps = jnp.stack([row_taps, row_taps[:, ::-1], column_taps, column_taps[:, ::-1]]).astype(jnp.float32)
    taps = jnp.pad(taps, ((0, 0), (0, 0), (0, WINDOW - tap_count)))

    vmem = pl.BlockSpec(memory_space=pltpu.VMEM)
    hbm = pl.BlockSpec(memory_space=pl.ANY)
    dims = (kernels, tap_count, strip, width, inner, outer)
    block = strip // 2 + inner
    bf16 = jnp.bfloat16
    residual, term = pl.pallas_call(
        functools.partial(filters_kernel, dims),
        out_shape=(
            jax.ShapeDtypeStruct((strip, width), jnp.float32),
            jax.ShapeDtypeStruct((strip, width), bf16),
        ),
        in_specs=[vmem, vmem, vmem, vmem, hbm, hbm, hbm],
        out_specs=(vmem, vmem),
        scratch_shapes=[
            pltpu.VMEM((kernels, strip + 2 * inner, width), bf16),
            pltpu.VMEM((strip + 2 * outer, width + LANES), bf16),
            pltpu.VMEM((kernels // 2, WINDOW, 2 * LANES), bf16),
            pltpu.VMEM((kernels, WINDOW, LANES), bf16),
            pltpu.VMEM((kernels, 2, block, WINDOW), bf16),
            pltpu.VMEM((kernels, 2, strip // 2, WINDOW), bf16),
            pltpu.VMEM((kernels, strip + 2 * outer, WINDOW), bf16),
            pltpu.VMEM((strip + 2 * inner, WINDOW), jnp.float32),
            pltpu.VMEM((kernels, strip, width), bf16),
            pltpu.VMEM((strip, width + LANES), jnp.float32),
            pltpu.SemaphoreType.DMA((width // WINDOW, 3)),
        ],
        compiler_params=pltpu.CompilerParams(vmem_limit_bytes=56 * 2**20),
        cost_estimate=pl.CostEstimate(flops=10**10, bytes_accessed=2 * 10**7, transcendentals=0),
    )(extended, taps, seen, mask, coefficients[0], above_coef, below_coef)

    incoming = lax.all_to_all(term[None], "exp", split_axis=2, concat_axis=0, tiled=True)
    owner = jnp.arange(ncells)[:, None] == cell_list[None, :]
    gradient = jnp.sum(
        jnp.where(owner[:, :, None, None], incoming[None].astype(jnp.float32), 0.0), axis=1)
    return (gradient, residual[None])


def fused_kernel(
    dims,
    cells_hbm, lat_hbm, along_hbm, down_hbm, valid_hbm, obs_hbm, coef_hbm,
    res_ref, grad_ref,
    cells_ref, lat_ref, along_ref, down_ref, valid_ref, cells, taps_ref, coef, seen, usable, outgoing, lat, lsh, fw, gw, ew, aw, bw, rb, resid, tot, stray, leaving, arrived,
    own_sems, lat_send, lat_recv, rim_send, rim_recv, halo_send, halo_recv, term_send, term_recv,
):
    count, row_count, kernels, tap_count, strip, width, inner, outer = dims
    half_width = tap_count // 2
    half = strip // 2
    block = half + inner
    chunks = width // WINDOW
    per = WINDOW // LANES
    me = lax.axis_index("exp")
    row = lax.axis_index("row")
    rising = me < count // 2
    has_above = row > 0
    has_below = row < row_count - 1

    def ordered(rank, length):
        return jnp.where(rising, rank, length - 1 - rank)

    def reversed_order(rank, length):
        return jnp.where(rising, length - 1 - rank, rank)

    def lane_block(b):
        return pl.ds(pl.multiple_of(b * LANES, LANES), LANES)

    def chunk_cols(c):
        return pl.ds(pl.multiple_of(c * WINDOW, WINDOW), WINDOW)

    barrier = pltpu.get_barrier_semaphore()
    for e in range(count):
        @pl.when(e != me)
        def _():
            pl.semaphore_signal(barrier, inc=1, device_id={"exp": e}, device_id_type=MESH)

    @pl.when(has_above)
    def _():
        pl.semaphore_signal(barrier, inc=1, device_id={"row": row - 1}, device_id_type=MESH)

    @pl.when(has_below)
    def _():
        pl.semaphore_signal(barrier, inc=1, device_id={"row": row + 1}, device_id_type=MESH)

    def own_coef(c):
        cols = chunk_cols(c)
        return pltpu.make_async_copy(
            coef_hbm.at[:, :, cols], coef.at[:, pl.ds(inner, strip), cols], own_sems.at[c])

    own_seen = pltpu.make_async_copy(obs_hbm, seen.at[pl.ds(inner, strip)], own_sems.at[chunks])
    fetched = [
        pltpu.make_async_copy(src, dst, own_sems.at[chunks + 1 + i])
        for i, (src, dst) in enumerate((
            (cells_hbm, cells_ref), (lat_hbm, lat_ref), (along_hbm, along_ref),
            (down_hbm, down_ref), (valid_hbm, valid_ref)))]
    for copy in fetched:
        copy.start()
    own_seen.start()
    for step in range(chunks):
        own_coef(ordered(step, chunks)).start()

    for copy in fetched:
        copy.wait()
    for e in range(count):
        cells[e] = jnp.broadcast_to(cells_ref[:, e:e + 1], (8, LANES))

    def owned(e, c):
        return jnp.concatenate([(cells[e] == c).astype(jnp.float32)] * (strip // 8), axis=0) > 0.5

    for e in range(count):
        chosen = lat_ref[0].astype(jnp.float32)
        for c in range(1, lat_ref.shape[0]):
            chosen = jnp.where(owned(e, c), lat_ref[c].astype(jnp.float32), chosen)
        outgoing[e] = chosen.astype(outgoing.dtype)
    at_row = lax.broadcasted_iota(jnp.int32, (strip, strip), 0)
    at_col = lax.broadcasted_iota(jnp.int32, (strip, strip), 1)
    spread = jnp.where(at_row == at_col, valid_ref[...], 0).astype(jnp.bfloat16)
    usable[pl.ds(inner, strip), :] = jnp.dot(
        spread, jnp.ones((strip, LANES), jnp.bfloat16),
        preferred_element_type=jnp.float32).astype(usable.dtype)
    for ref in (lat,):
        ref[:, pl.ds(0, LANES)] = jnp.zeros((ref.shape[0], LANES), ref.dtype)
        ref[:, pl.ds(LANES + width, LANES)] = jnp.zeros((ref.shape[0], LANES), ref.dtype)

    def fill(at_lat, at_inner):
        lat[pl.ds(at_lat, outer), :] = jnp.zeros((outer, lat.shape[1]), lat.dtype)
        coef[:, pl.ds(at_inner, inner), :] = jnp.zeros((kernels, inner, width), coef.dtype)
        seen[pl.ds(at_inner, inner), :] = jnp.zeros((inner, width), seen.dtype)
        usable[pl.ds(at_inner, inner), :] = jnp.zeros((inner, LANES), usable.dtype)

    @pl.when(jnp.logical_not(has_above))
    def _():
        fill(0, 0)

    @pl.when(jnp.logical_not(has_below))
    def _():
        fill(outer + strip, inner + strip)

    pl.semaphore_wait(barrier, count - 1 + has_above.astype(jnp.int32) + has_below.astype(jnp.int32))

    strip_rows = pl.ds(outer, strip)

    def lat_copy(e):
        return pltpu.make_async_remote_copy(
            src_ref=outgoing.at[e], dst_ref=lat.at[strip_rows, lane_block(me + 1)],
            send_sem=lat_send.at[e], recv_sem=lat_recv.at[me],
            device_id={"exp": e}, device_id_type=MESH)

    def own_lat():
        return pltpu.make_async_copy(
            outgoing.at[me], lat.at[strip_rows, lane_block(me + 1)], lat_recv.at[me])

    def halo_copies(c, side):
        cols = chunk_cols(c)
        source = pl.ds(0 if side == 0 else strip - inner, inner)
        target = pl.ds(inner + strip if side == 0 else 0, inner)
        return pltpu.make_async_remote_copy(
            src_ref=coef_hbm.at[:, source, cols], dst_ref=coef.at[:, target, cols],
            send_sem=halo_send.at[side, c], recv_sem=halo_recv.at[side, c],
            device_id={"row": row - 1 if side == 0 else row + 1}, device_id_type=MESH)

    def seen_copies(side):
        source = 0 if side == 0 else strip - inner
        target = pl.ds(inner + strip if side == 0 else 0, inner)
        return [pltpu.make_async_remote_copy(
            src_ref=src.at[pl.ds(first + source, inner)], dst_ref=dst.at[target],
            send_sem=halo_send.at[side, chunks + i], recv_sem=halo_recv.at[side, chunks + i],
            device_id={"row": row - 1 if side == 0 else row + 1}, device_id_type=MESH)
            for i, (src, first, dst) in enumerate(((obs_hbm, 0, seen), (usable, inner, usable)))]

    def rim_copy(b, side):
        cols = lane_block(b + 1)
        source = pl.ds(outer if side == 0 else strip, outer)
        target = pl.ds(outer + strip if side == 0 else 0, outer)
        return pltpu.make_async_remote_copy(
            src_ref=lat.at[source, cols], dst_ref=lat.at[target, cols],
            send_sem=rim_send.at[side, b], recv_sem=rim_recv.at[side, b],
            device_id={"row": row - 1 if side == 0 else row + 1}, device_id_type=MESH)

    sends = ((0, has_above), (1, has_below))
    receives = ((0, has_below), (1, has_above))

    def start_halos(step):
        for side, there in sends:
            @pl.when(there)
            def _():
                halo_copies(ordered(step, chunks), side).start()

    late = ordered(me, count) < count // 4
    own_lat().start()
    for rank in range(count):
        e = ordered(rank, count)
        @pl.when(jnp.logical_and(e != me, jnp.logical_or(jnp.logical_not(late), rank < count // 2)))
        def _():
            lat_copy(e).start()
    start_halos(0)
    for side, there in sends:
        @pl.when(there)
        def _():
            for copy in seen_copies(side):
                copy.start()

    low_a = strip + 2 * outer - WINDOW
    low_b = strip + 2 * inner - WINDOW
    shift = LANES // 2 + half_width

    at_tap = lax.broadcasted_iota(jnp.int32, (tap_count, WINDOW), 0)
    at_lane = lax.broadcasted_iota(jnp.int32, (tap_count, WINDOW), 1)
    keep = (at_tap == at_lane).astype(jnp.float32).astype(jnp.bfloat16)
    turn = (at_tap + at_lane == tap_count - 1).astype(jnp.float32).astype(jnp.bfloat16)
    for i, (taps, order) in enumerate(((along_ref, keep), (along_ref, turn), (down_ref, keep), (down_ref, turn))):
        taps_ref[i] = jnp.dot(taps[...], order, preferred_element_type=jnp.float32)

    far = (
        lax.broadcasted_iota(jnp.int32, (WINDOW, WINDOW), 0)
        - lax.broadcasted_iota(jnp.int32, (WINDOW, WINDOW), 1))
    corner = jnp.abs(far) >= LANES

    @pl.loop(0, kernels // 2)
    def _(pair):
        for odd in range(2):
            k = 2 * pair + odd
            along = taps_ref[0, pl.ds(k, 1), :]
            along_rev = taps_ref[1, pl.ds(k, 1), :]
            down = taps_ref[2, pl.ds(k, 1), :]
            down_rev = taps_ref[3, pl.ds(k, 1), :]
            fw[pair, :, pl.ds(odd * LANES, LANES)] = toeplitz(along_rev, WINDOW, -shift)[:, :LANES].astype(fw.dtype)
            ring = toeplitz(along, WINDOW, -half_width)
            gw[k] = jnp.where(corner, 0.0, ring).astype(gw.dtype)
            reach = jnp.where(corner, ring, 0.0)
            reach = reach[:, :LANES] + reach[:, LANES:]
            ew[pair, pl.ds(odd * LANES, LANES // 2), :] = reach[:LANES // 2].astype(ew.dtype)
            ew[pair, pl.ds(odd * LANES + LANES // 2, LANES // 2), :] = reach[WINDOW - LANES // 2:].astype(ew.dtype)
            aw[k, 0] = toeplitz(down, block, outer - inner - half_width).astype(aw.dtype)
            aw[k, 1] = toeplitz(down, block, half + outer - half_width - low_a).astype(aw.dtype)
            bw[k, 0] = toeplitz(down_rev, half, inner - half_width).astype(bw.dtype)
            bw[k, 1] = toeplitz(down_rev, half, half + inner - half_width - low_b).astype(bw.dtype)

    for at in (0, chunks + 1):
        stray[at] = jnp.zeros((strip, LANES), stray.dtype)

    def take_block(rank):
        b = ordered(rank, count)
        pltpu.make_async_copy(
            outgoing.at[0], lat.at[strip_rows, lane_block(b + 1)], lat_recv.at[b]).wait()
        for side, there in sends:
            @pl.when(there)
            def _():
                rim_copy(b, side).start()

    def take_rims(rank):
        b = ordered(rank, count)
        for side, there in receives:
            @pl.when(there)
            def _():
                rim_copy(b, side).wait_recv()

    for rank in range(count // 2, count):
        @pl.when(late)
        def _():
            lat_copy(ordered(rank, count)).start()
    for rank in range(per + 1):
        take_block(rank)
    own_seen.wait()
    for side, there in receives:
        @pl.when(there)
        def _():
            for copy in seen_copies(side):
                copy.wait_recv()
    take_rims(0)

    @pl.loop(0, chunks)
    def _(step):
        c = ordered(step, chunks)
        cols = chunk_cols(c)

        @pl.when(step + 1 < chunks)
        def _():
            start_halos(step + 1)

        for more in range(1, per + 1):
            @pl.when(step * per + more < count)
            def _():
                take_rims(step * per + more)
        near = lat[:, pl.ds(pl.multiple_of(c * WINDOW, WINDOW), WINDOW + 2 * LANES)]
        lsh[...] = near[:, LANES // 2:LANES // 2 + WINDOW + LANES]
        for b in range(per):
            window = lsh[:, pl.ds(b * LANES, WINDOW)]
            for pair in range(kernels // 2):
                both = jnp.dot(window, fw[pair], preferred_element_type=jnp.float32).astype(rb.dtype)
                rb[2 * pair, :, pl.ds(b * LANES, LANES)] = both[:, :LANES]
                rb[2 * pair + 1, :, pl.ds(b * LANES, LANES)] = both[:, LANES:]
        own_coef(c).wait()
        for side, there in receives:
            @pl.when(there)
            def _():
                halo_copies(c, side).wait_recv()
        for part in range(2):
            if part == 1:
                for more in range(1, per + 1):
                    @pl.when((step + 1) * per + more < count)
                    def _():
                        take_block((step + 1) * per + more)
            rows = pl.ds(part * block, block)
            reach = pl.ds(part * low_a, WINDOW)
            predicted = jnp.zeros((block, WINDOW), jnp.float32)
            for k in range(kernels):
                vertical = jnp.dot(aw[k, part], rb[k, reach, :], preferred_element_type=jnp.float32)
                predicted += coef[k, rows, cols].astype(jnp.float32) * vertical
            mask = usable[rows, :].astype(jnp.float32)
            mask = jnp.concatenate([mask] * per, axis=1)
            resid[rows, cols] = mask * (predicted - seen[rows, cols].astype(jnp.float32))
        res_ref[:, cols] = resid[pl.ds(inner, strip), cols]

    def term_copy(b):
        return pltpu.make_async_remote_copy(
            src_ref=leaving.at[b], dst_ref=arrived.at[me],
            send_sem=term_send.at[b], recv_sem=term_recv.at[me],
            device_id={"exp": b}, device_id_type=MESH)

    lane_side = lax.broadcasted_iota(jnp.int32, (strip, LANES), 1) // (LANES // 2)

    def send_term(rank):
        b = reversed_order(rank, count)
        c, side = b // per, b % per
        beside = stray[jnp.where(side == 0, c, c + 2)]
        term = tot[:, lane_block(b)] + jnp.where(lane_side == side, beside, 0.0)
        leaving[b] = term.astype(leaving.dtype)

        @pl.when(b != me)
        def _():
            term_copy(b).start()

    @pl.loop(0, chunks)
    def _(step):
        c = reversed_order(step, chunks)
        cols = chunk_cols(c)
        inside = jnp.zeros((strip, WINDOW), jnp.float32)
        outside = jnp.zeros((strip, LANES), jnp.float32)
        left = lax.broadcasted_iota(jnp.int32, (strip, LANES), 1) < LANES // 2
        for group in range(kernels // GROUP):
            backs, edges = [], []
            for odd in range(GROUP):
                k = GROUP * group + odd
                weighted = (coef[k, :, cols].astype(jnp.float32) * resid[:, cols]).astype(jnp.bfloat16)
                back = jnp.concatenate([
                    jnp.dot(
                        bw[k, part], weighted[part * low_b:part * low_b + WINDOW],
                        preferred_element_type=jnp.float32).astype(jnp.bfloat16)
                    for part in range(2)], axis=0)
                backs.append(back)
                edges.append(jnp.where(left, back[:, :LANES], back[:, LANES:]))
            inside += jnp.dot(
                jnp.concatenate(backs, axis=1),
                gw[GROUP * group:GROUP * (group + 1)].reshape(GROUP * WINDOW, WINDOW),
                preferred_element_type=jnp.float32)
            outside += jnp.dot(
                jnp.concatenate(edges, axis=1),
                ew[GROUP // 2 * group:GROUP // 2 * (group + 1)].reshape(GROUP * LANES, LANES),
                preferred_element_type=jnp.float32)
        tot[:, cols] = inside
        stray[c + 1] = outside

        @pl.when(step > 0)
        def _():
            send_term(step * per - 1)

        send_term(step * per)

    send_term(count - 1)

    for c in range(grad_ref.shape[0]):
        grad_ref[c] = jnp.where(owned(me, c), leaving[me].astype(jnp.float32), 0.0)
    for rank in range(count):
        e = reversed_order(rank, count)

        @pl.when(e != me)
        def _():
            pltpu.make_async_copy(leaving.at[0], arrived.at[e], term_recv.at[e]).wait()
            value = arrived[e].astype(jnp.float32)
            for c in range(grad_ref.shape[0]):
                grad_ref[c] += jnp.where(owned(e, c), value, 0.0)

    for e in range(count):
        @pl.when(e != me)
        def _():
            lat_copy(e).wait_send()
            term_copy(e).wait_send()
    for side, there in sends:
        @pl.when(there)
        def _():
            for copy in seen_copies(side):
                copy.wait_send()
            for c in range(chunks):
                halo_copies(c, side).wait_send()
            for b in range(count):
                rim_copy(b, side).wait_send()


def fused_body(latent, row_taps, column_taps, coefficients, observed, cell_of, valid_rows):
    kernels, tap_count = row_taps.shape
    half_width = tap_count // 2
    strip, width = observed.shape[1:]
    ncells = latent.shape[0]
    inner = round_up(half_width, PACK)
    outer = round_up(2 * half_width, PACK)
    count, row_count = lax.axis_size("exp"), lax.axis_size("row")

    vmem = pl.BlockSpec(memory_space=pltpu.VMEM)
    hbm = pl.BlockSpec(memory_space=pltpu.HBM)
    chunks = width // WINDOW
    block = strip // 2 + inner
    bf16 = jnp.bfloat16
    dma = pltpu.SemaphoreType.DMA
    dims = (count, row_count, kernels, tap_count, strip, width, inner, outer)
    residual, gradient = pl.pallas_call(
        functools.partial(fused_kernel, dims),
        out_shape=(
            jax.ShapeDtypeStruct((strip, width), jnp.float32),
            jax.ShapeDtypeStruct((ncells, strip, LANES), jnp.float32),
        ),
        in_specs=[hbm] * 7,
        out_specs=(vmem, vmem),
        scratch_shapes=[
            pltpu.VMEM((1, count), jnp.int32),
            pltpu.VMEM((ncells, strip, LANES), bf16),
            pltpu.VMEM((kernels, tap_count), bf16),
            pltpu.VMEM((kernels, tap_count), bf16),
            pltpu.VMEM((1, strip), jnp.int32),
            pltpu.VMEM((count, 8, LANES), jnp.int32),
            pltpu.VMEM((4, kernels, WINDOW), jnp.float32),
            pltpu.VMEM((kernels, strip + 2 * inner, width), bf16),
            pltpu.VMEM((strip + 2 * inner, width), bf16),
            pltpu.VMEM((strip + 2 * inner, LANES), bf16),
            pltpu.VMEM((count, strip, LANES), bf16),
            pltpu.VMEM((strip + 2 * outer, width + 2 * LANES), bf16),
            pltpu.VMEM((strip + 2 * outer, WINDOW + LANES), bf16),
            pltpu.VMEM((kernels // 2, WINDOW, 2 * LANES), bf16),
            pltpu.VMEM((kernels, WINDOW, WINDOW), bf16),
            pltpu.VMEM((kernels // 2, WINDOW, LANES), bf16),
            pltpu.VMEM((kernels, 2, block, WINDOW), bf16),
            pltpu.VMEM((kernels, 2, strip // 2, WINDOW), bf16),
            pltpu.VMEM((kernels, strip + 2 * outer, WINDOW), bf16),
            pltpu.VMEM((strip + 2 * inner, width), jnp.float32),
            pltpu.VMEM((strip, width), jnp.float32),
            pltpu.VMEM((chunks + 2, strip, LANES), jnp.float32),
            pltpu.VMEM((count, strip, LANES), bf16),
            pltpu.VMEM((count, strip, LANES), bf16),
            dma((chunks + 6,)),
            dma((count,)), dma((count,)),
            dma((2, count)), dma((2, count)),
            dma((2, chunks + 2)), dma((2, chunks + 2)),
            dma((count,)), dma((count,)),
        ],
        compiler_params=pltpu.CompilerParams(
            vmem_limit_bytes=44 * 2**20, collective_id=0, has_side_effects=True),
        cost_estimate=pl.CostEstimate(flops=10**10, bytes_accessed=2 * 10**7, transcendentals=0),
    )(*[pltpu.with_memory_space_constraint(x, pltpu.HBM) for x in (
        cell_of.reshape(1, count), latent, row_taps, column_taps, valid_rows, observed[0], coefficients[0])])
    return (gradient, residual[None])


def body(latent, *others):
    if latent.shape[2] == LANES:
        return fused_body(latent, *others)
    return apart_body(latent, *others)


def solution(mesh):
    placed = (
        P(None, "row", "exp"),
        P(),
        P(),
        P("exp", None, "row", None),
        P("exp", "row", None),
        P(),
        P("exp", "row"),
    )
    return jax.shard_map(
        body,
        mesh=mesh,
        in_specs=placed,
        out_specs=(P(None, "row", "exp"), P("exp", "row", None)),
        check_vma=False,
    )
```
